128 devices in a mesh: ctx: 32 (over z, x, core), ch: 4 (over y).
Axes of the slice: x: 4, y: 4, z: 4, core: 2. Of those that a mesh axis runs over, the one named last changes fastest.
Arguments:
- projections: bfloat16 [3, 4096, 8192], P(None, 'ch', 'ctx'), may hold values from -6 to 6
- short_filter: float32 [3, 4096, 3], P(None, 'ch'), may hold values from -3 to 3
- skip_gain: float32 [4096], P('ch'), may hold values from -1 to 1
- filter_spectra: bfloat16 [2, 4096, 16384], P(None, 'ch', 'ctx'), may hold values from -6 to 6
Outputs:
- gated_output: bfloat16 [4096, 8192], P('ch', 'ctx')
The draws below stay inside these ranges and needn't reach their ends.
All inputs are finite; a program needn't handle non-finite values.
Results may differ from the reference program's by a relative error of at most 0.0075.
Values may be sent and summed in bfloat16 or wider, within the bound.
A program may use at most 128 MiB of HBM per device.

```python
import math
import jax
import jax.numpy as jnp
from jax import lax

CH = 4096
SHORT = 3
TOKENS = 8192
FREQS = 16384


def block_scale(stream_key, extent, cuts, smallest, high):
    gain, own = 1.0, jax.random.fold_in(stream_key, 6)
    for axis_at, parts in cuts:
        draws = jnp.exp(jax.random.uniform(jax.random.fold_in(own, axis_at), (parts,), jnp.float32, smallest / len(cuts), high / len(cuts)))
        gain = gain * jnp.repeat(draws, extent[axis_at] // parts).reshape([-1 if axis == axis_at else 1 for axis in range(len(extent))])
    return gain


def gaussian(own_key, shape, deviation, limit, cuts=(), kind=jnp.bfloat16):
    level = block_scale(own_key, shape, cuts, -0.22, 0.18) if cuts else 1.0
    values = jax.random.normal(own_key, shape, jnp.float32) * deviation * level
    return jnp.minimum(jnp.maximum(values, -limit), limit).astype(kind)


def setup_inputs(seed: int = 0) -> dict:
    splits = jax.random.split(jax.random.key(seed), 5)
    projections = gaussian(splits[0], (3, CH, TOKENS), 1.0, 6.0, ((1, 4), (2, 32)))
    short_filter = gaussian(splits[1], (3, CH, SHORT), 0.6, 3.0, ((1, 4),), jnp.float32)
    skip_gain = jnp.clip(jax.random.uniform(splits[2], (CH,), jnp.float32, -1.0, 1.0) * block_scale(splits[2], (CH,), ((0, 4),), -0.4, 0.0), -1.0, 1.0)
    filter_spectra = gaussian(splits[3], (2, CH, FREQS), 1.0, 6.0, ((1, 4), (2, 32)))
    return {"projections": projections, "short_filter": short_filter, "skip_gain": skip_gain, "filter_spectra": filter_spectra}


def reference(projections, short_filter, skip_gain, filter_spectra):
    group = math.gcd(CH, 256)
    count = CH // group

    def one_group(index):
        start = index * group
        proj = lax.dynamic_slice_in_dim(projections, start, group, 1).astype(jnp.float32)
        taps = lax.dynamic_slice_in_dim(short_filter, start, group, 1)
        gains = lax.dynamic_slice_in_dim(skip_gain, start, group, 0)
        spectra = lax.dynamic_slice_in_dim(filter_spectra, start, group, 1)
        padded = jnp.pad(proj, ((0, 0), (0, 0), (2, 0)))
        filtered = taps[:, :, 0:1] * padded[:, :, 2:] + taps[:, :, 1:2] * padded[:, :, 1:-1] + taps[:, :, 2:3] * padded[:, :, :-2]
        query = filtered[0]
        product = (filtered[1] * filtered[2]).astype(jnp.bfloat16)
        wide = product.astype(jnp.float32)
        extended = jnp.concatenate([wide, jnp.zeros_like(wide)], axis=1)
        spectrum = jnp.fft.fft(extended, axis=1)
        filter_complex = spectra[0].astype(jnp.float32) + 1j * spectra[1].astype(jnp.float32)
        shaped = spectrum * filter_complex
        long_conv = jnp.real(jnp.fft.ifft(shaped, axis=1))[:, :TOKENS]
        result = query * (long_conv + gains[:, None] * wide)
        return result.astype(jnp.bfloat16)

    pieces = lax.map(one_group, jnp.arange(count, dtype=jnp.int32))
    return pieces.reshape(CH, TOKENS)
```

```python
import functools

import jax
import jax.numpy as jnp
import ml_dtypes
import numpy as np
from jax import lax
from jax.experimental import pallas as pl
from jax.experimental.pallas import tpu as pltpu
from jax.sharding import PartitionSpec as P

MESH = pl.DeviceIdType.MESH
SIDE = 128
GROUP = 8
f32, bf16 = jnp.float32, jnp.bfloat16


def tables(n, own, s_lo, a_lo):
    period = SIDE * SIDE
    groups = own // GROUP
    cols = 2 * a_lo
    order_f = np.zeros((own * cols, own * cols))
    c, j = np.meshgrid(np.arange(own), np.arange(cols), indexing="ij")
    order_f[(c * cols + j).ravel(), (j * own + c).ravel()] = 1
    order_x = np.zeros((SIDE * s_lo, SIDE * s_lo))
    c, s = np.meshgrid(np.arange(SIDE), np.arange(s_lo), indexing="ij")
    order_x[(c * s_lo + s).ravel(), (s * SIDE + c).ravel()] = 1
    order_y = np.zeros((SIDE * s_lo, SIDE * s_lo))
    pairs = SIDE // GROUP
    q, c, s = np.meshgrid(np.arange(pairs), np.arange(GROUP), np.arange(s_lo), indexing="ij")
    order_y[(s * SIDE + q * GROUP + c).ravel(), ((q * GROUP + c) * s_lo + s).ravel()] = 1
    q, part, al = (v.ravel() for v in np.meshgrid(np.arange(n), np.arange(2), np.arange(a_lo), indexing="ij"))
    angle = 2 * np.pi * ((q * a_lo + al)[:, None] * np.arange(SIDE)[None, :] % SIDE) / SIDE
    wr, wi = np.cos(angle), -np.sin(angle)
    sign = np.where(part == 1, -1.0, 1.0)[:, None]
    forward = np.concatenate([np.concatenate([wr, -wi], 1), np.concatenate([wi, wr], 1) * sign], 0)
    vr, vi = np.cos(angle).T, np.sin(angle).T
    real = (part == 0)[None, :]
    inverse = np.concatenate([np.where(real, vr, -vi), np.where(real, vi, vr)], 0)
    small = np.concatenate([order_f, order_x, order_y, forward, inverse], 0)
    s = np.arange(n * s_lo)
    angle = 2 * np.pi * (s[:, None] * np.arange(SIDE)[None, :] % SIDE) / SIDE
    first = np.zeros((n, GROUP, s_lo, GROUP, 2, SIDE))
    last = np.zeros((n, GROUP, s_lo, GROUP, 2, SIDE))
    for g in range(GROUP):
        first[:, g, :, g, 0] = np.cos(angle).reshape(n, s_lo, SIDE)
        first[:, g, :, g, 1] = -np.sin(angle).reshape(n, s_lo, SIDE)
        last[:, g, :, g, 0] = np.cos(angle).reshape(n, s_lo, SIDE) / period
        last[:, g, :, g, 1] = -np.sin(angle).reshape(n, s_lo, SIDE) / period
    shape = (n * GROUP * s_lo, GROUP * 2 * SIDE)
    angle = 2 * np.pi * np.arange(SIDE)[:, None] * np.arange(SIDE)[None, :] / period
    twiddle = np.concatenate([np.cos(angle), np.sin(angle)], 0)
    tail = np.zeros((3, 16, SIDE))
    edge = np.zeros((16, 3, 2, SIDE))
    for e in range(3):
        tail[e, 2 * e, SIDE - 2] = 1
        tail[e, 2 * e + 1, SIDE - 1] = 1
        edge[2 * e + 1, e, 0, 0] = 1
        edge[2 * e, e, 1, 0] = 1
        edge[2 * e + 1, e, 1, 1] = 1
    return [
        small.astype(ml_dtypes.bfloat16),
        twiddle.astype(np.float32),
        first.reshape(shape).astype(ml_dtypes.bfloat16),
        last.reshape(shape).astype(ml_dtypes.bfloat16),
        tail.reshape(48, SIDE).astype(ml_dtypes.bfloat16),
        edge.reshape(16, 6 * SIDE).astype(ml_dtypes.bfloat16),
    ]


def peer(me, o):
    z, x, c = me // 8, (me // 2) % 4, me % 2
    return (z + o // 8) % 4 * 8 + (x + o // 2) % 4 * 2 + (c + o) % 2


def dot(a, b):
    return jnp.dot(a, b, preferred_element_type=f32)


def dot_nt(a, b):
    return lax.dot_general(a, b, (((1,), (1,)), ((), ())), preferred_element_type=f32)


def dot_tn(a, b):
    return lax.dot_general(a, b, (((0,), (0,)), ((), ())), preferred_element_type=f32)


def kernel(
    n, own, s_lo, a_lo,
    filt_hbm, proj_hbm, taps_hbm, skip, small_hbm, twiddle_hbm, first_hbm, last_hbm, tail, edge,
    out,
    filt, proj, taps, small, twiddle, first, last,
    fsend, fbuf, xsend, xbuf, ysend, ybuf, spec, back, conv, query, direct, halo_out, halo_in,
    load_sem, own_sem, fsend_sem, frecv_sem, xsend_sem, xrecv_sem, ysend_sem, yrecv_sem, hsend_sem, hrecv_sem,
):
    me = lax.axis_index("ctx")
    groups = own // GROUP
    cols = 2 * a_lo
    xrows = GROUP * s_lo
    frows = GROUP * cols
    blocks = n * own // SIDE
    per_block = SIDE // own

    loads = [
        pltpu.make_async_copy(src, dst, load_sem.at[i])
        for i, (src, dst) in enumerate(
            [(small_hbm, small), (filt_hbm, filt), (proj_hbm, proj), (taps_hbm, taps), (twiddle_hbm, twiddle), (first_hbm, first), (last_hbm, last)]
        )
    ]
    for load in loads:
        load.start()

    barrier = pltpu.get_barrier_semaphore()

    def greet(i, carry):
        pl.semaphore_signal(barrier, inc=1, device_id={"ctx": peer(me, i)}, device_id_type=MESH)
        return carry

    lax.fori_loop(1, n, greet, 0)

    order_f = small.at[pl.ds(0, 256)]
    order_x = small.at[pl.ds(256, 256)]
    order_y = small.at[pl.ds(512, 256)]
    forward = small.at[pl.ds(768, 512)]
    inverse = small.at[pl.ds(1280, 256)]

    loads[0].wait()
    loads[1].wait()

    def arrange(d, carry):
        rows = pl.ds(pl.multiple_of(d * own, own), own)
        stacked = jnp.concatenate(
            [filt[part, rows, al * SIDE : (al + 1) * SIDE] for part in range(2) for al in range(a_lo)], axis=0
        )
        fsend[d] = dot(order_f[...], stacked).astype(bf16)
        return carry

    lax.fori_loop(0, n, arrange, 0)
    own_f = pltpu.make_async_copy(fsend.at[me], fbuf.at[me], own_sem.at[0])
    own_f.start()

    loads[2].wait()
    halo_out[...] = sum(
        dot_nt(tail[16 * e : 16 * e + 16, :], proj[e, :, (s_lo - 1) * SIDE : s_lo * SIDE]) for e in range(3)
    ).astype(bf16)

    pl.semaphore_wait(barrier, n - 1)

    halo = pltpu.make_async_remote_copy(
        src_ref=halo_out, dst_ref=halo_in, send_sem=hsend_sem, recv_sem=hrecv_sem,
        device_id={"ctx": (me + 1) % n}, device_id_type=MESH,
    )
    halo.start()

    def f_copy(g, d):
        rows = pl.ds(pl.multiple_of(g * frows, frows), frows)
        return pltpu.make_async_remote_copy(
            src_ref=fsend.at[d, rows], dst_ref=fbuf.at[me, rows], send_sem=fsend_sem.at[g], recv_sem=frecv_sem.at[g],
            device_id={"ctx": d}, device_id_type=MESH,
        )

    def f_all(g):
        rows = pl.ds(pl.multiple_of(g * frows, frows), frows)
        return pltpu.make_async_remote_copy(
            src_ref=fsend.at[pl.ds(0, n - 1), rows], dst_ref=fbuf.at[pl.ds(0, n - 1), rows],
            send_sem=fsend_sem.at[g], recv_sem=frecv_sem.at[g], device_id={"ctx": (me + 1) % n}, device_id_type=MESH,
        )

    def f_start(g):
        def one(i, carry):
            f_copy(g, peer(me, i * 11 % n)).start()
            return carry

        lax.fori_loop(1, n, one, 0)

    f_start(0)

    loads[3].wait()
    halo.wait_recv()
    lane = lax.broadcasted_iota(jnp.int32, (SIDE, SIDE), 1)
    eye = lax.broadcasted_iota(jnp.int32, (SIDE, SIDE), 0) == lane
    inside = jnp.where(me == 0, 0.0, 1.0).astype(f32)

    def gate(blk, carry):
        rows = pl.ds(pl.multiple_of(blk * SIDE, SIDE), SIDE)
        edges = dot_tn(halo_in[:, rows], edge[...]) * inside
        filtered = []
        for e in range(3):
            x = proj[e, rows, :].astype(f32)
            back1, back2 = pltpu.roll(x, 1, 1), pltpu.roll(x, 2, 1)
            at = 2 * SIDE * e
            back1 = jnp.concatenate([jnp.where(lane < 1, edges[:, at : at + SIDE], back1[:, :SIDE]), back1[:, SIDE:]], axis=1)
            back2 = jnp.concatenate(
                [jnp.where(lane < 2, edges[:, at + SIDE : at + 2 * SIDE], back2[:, :SIDE]), back2[:, SIDE:]], axis=1
            )
            tap = taps[e, rows, :]
            filtered.append(tap[:, 0:1] * x + tap[:, 1:2] * back1 + tap[:, 2:3] * back2)
        product = (filtered[1] * filtered[2]).astype(bf16)
        gain = jnp.sum(jnp.where(eye, skip[pl.ds(blk, 1), :], 0.0), axis=1, keepdims=True)
        query[rows, :] = filtered[0]
        direct[rows, :] = gain * product.astype(f32)
        stacked = jnp.concatenate([product[:, s * SIDE : (s + 1) * SIDE] for s in range(s_lo)], axis=0)
        arranged = dot(order_x[...], stacked).astype(bf16)
        xsend[pl.ds(pl.multiple_of(blk * per_block, per_block), per_block)] = arranged.reshape(per_block, own * s_lo, SIDE)
        return carry

    lax.fori_loop(0, blocks, gate, 0)

    def x_copy(d):
        return pltpu.make_async_remote_copy(
            src_ref=xsend.at[d], dst_ref=xbuf.at[me], send_sem=xsend_sem, recv_sem=xrecv_sem,
            device_id={"ctx": d}, device_id_type=MESH,
        )

    x_all = pltpu.make_async_remote_copy(
        src_ref=xsend.at[pl.ds(0, n - 1)], dst_ref=xbuf.at[pl.ds(0, n - 1)], send_sem=xsend_sem, recv_sem=xrecv_sem,
        device_id={"ctx": (me + 1) % n}, device_id_type=MESH,
    )

    def x_start(i, carry):
        x_copy(peer(me, i * 11 % n)).start()
        return carry

    lax.fori_loop(1, n, x_start, 0)
    own_x = pltpu.make_async_copy(xsend.at[me], xbuf.at[me], own_sem.at[1])
    own_x.start()

    for g in range(1, groups):
        f_start(g)

    for load in loads[4:]:
        load.wait()
    own_x.wait()
    x_all.wait_recv()
    cos, sin = twiddle[0:SIDE, :], twiddle[SIDE : 2 * SIDE, :]

    for g in range(groups):
        turned = xbuf[:, g * xrows : (g + 1) * xrows, :].reshape(n * xrows, SIDE).T

        def over_s(cp, carry, g=g, turned=turned):
            part = dot(turned, first[:, pl.ds(pl.multiple_of(cp * 4 * SIDE, 4 * SIDE), 4 * SIDE)])
            for c in range(2):
                re, im = part[:, 2 * c * SIDE : (2 * c + 1) * SIDE], part[:, (2 * c + 1) * SIDE : (2 * c + 2) * SIDE]
                spec[g * GROUP // 2 + cp, 0:SIDE, c * SIDE : (c + 1) * SIDE] = (re * cos + im * sin).astype(bf16)
                spec[g * GROUP // 2 + cp, SIDE : 2 * SIDE, c * SIDE : (c + 1) * SIDE] = (im * cos - re * sin).astype(bf16)
            return carry

        lax.fori_loop(0, GROUP // 2, over_s, 0)

    own_f.wait()
    half = n * cols

    def y_copy(g, d):
        return pltpu.make_async_remote_copy(
            src_ref=ysend.at[g, pl.ds(pl.multiple_of(d * xrows, xrows), xrows)],
            dst_ref=ybuf.at[g, pl.ds(pl.multiple_of(me * xrows, xrows), xrows)],
            send_sem=ysend_sem.at[g], recv_sem=yrecv_sem.at[g], device_id={"ctx": d}, device_id_type=MESH,
        )

    def y_all(g):
        return pltpu.make_async_remote_copy(
            src_ref=ysend.at[g, pl.ds(0, (n - 1) * xrows)], dst_ref=ybuf.at[g, pl.ds(0, (n - 1) * xrows)],
            send_sem=ysend_sem.at[g], recv_sem=yrecv_sem.at[g], device_id={"ctx": (me + 1) % n}, device_id_type=MESH,
        )

    own_y = []
    for g in range(groups):
        f_all(g).wait_recv()

        def through(cp, carry, g=g):
            values = dot(forward[...], spec[g * GROUP // 2 + cp])
            taken = fbuf[:, pl.ds(pl.multiple_of(g * frows + cp * 2 * cols, 2 * cols), 2 * cols), :].astype(f32)
            shaped = []
            for c in range(2):
                gains = taken[:, c * cols : (c + 1) * cols, :]
                straight = values[:half, c * SIDE : (c + 1) * SIDE].reshape(n, cols, SIDE) * gains
                crossed = values[half:, c * SIDE : (c + 1) * SIDE].reshape(n, cols, SIDE) * gains
                shaped.append((straight + pltpu.roll(crossed, a_lo, 1)).reshape(half, SIDE).astype(bf16))
            values = dot(inverse[...], jnp.concatenate(shaped, axis=1))
            for c in range(2):
                re, im = values[:SIDE, c * SIDE : (c + 1) * SIDE], values[SIDE:, c * SIDE : (c + 1) * SIDE]
                at = pl.multiple_of(cp * 4 * SIDE, 4 * SIDE) + 2 * c * SIDE
                back[:, pl.ds(pl.multiple_of(at, SIDE), SIDE)] = (re * cos - im * sin).astype(bf16)
                back[:, pl.ds(pl.multiple_of(at + SIDE, SIDE), SIDE)] = (re * sin + im * cos).astype(bf16)
            return carry

        lax.fori_loop(0, GROUP // 2, through, 0)
        ysend[g] = dot_nt(last[...], back[...]).astype(bf16)

        def y_start(i, carry, g=g):
            y_copy(g, peer(me, i * 11 % n)).start()
            return carry

        lax.fori_loop(1, n, y_start, 0)
        mine = pl.ds(pl.multiple_of(me * xrows, xrows), xrows)
        own_y.append(pltpu.make_async_copy(ysend.at[g, mine], ybuf.at[g, mine], own_sem.at[2 + g]))
        own_y[g].start()

    pairs = SIDE // GROUP
    for g in range(groups):
        own_y[g].wait()
        y_all(g).wait_recv()
        for h in range(n // pairs):
            arranged = dot(order_y[...], ybuf[g, h * pairs * xrows : (h + 1) * pairs * xrows, :])
            for s in range(s_lo):
                conv[h * pairs : (h + 1) * pairs, g * GROUP : (g + 1) * GROUP, s * SIDE : (s + 1) * SIDE] = arranged[
                    s * SIDE : (s + 1) * SIDE, :
                ].reshape(pairs, GROUP, SIDE)

    def finish(blk, carry):
        rows = pl.ds(pl.multiple_of(blk * SIDE, SIDE), SIDE)
        values = conv[pl.ds(pl.multiple_of(blk * per_block, per_block), per_block)].reshape(SIDE, s_lo * SIDE)
        out[rows, :] = (query[rows, :] * (values + direct[rows, :])).astype(bf16)
        return carry

    lax.fori_loop(0, blocks, finish, 0)

    halo.wait_send()
    x_all.wait_send()
    for g in range(groups):
        f_all(g).wait_send()
        y_all(g).wait_send()


def shards(projections, short_filter, skip_gain, filter_spectra):
    n = lax.axis_size("ctx")
    channels, tokens = projections.shape[1:]
    freqs = filter_spectra.shape[2]
    own, s_lo, a_lo = channels // n, tokens // SIDE, freqs // SIDE
    groups = own // GROUP
    cols = 2 * a_lo
    anywhere, vmem = pl.BlockSpec(memory_space=pl.ANY), pl.BlockSpec(memory_space=pltpu.VMEM)
    small, twiddle, first, last, tail, edge = tables(n, own, s_lo, a_lo)
    dma = pltpu.SemaphoreType.DMA
    return pl.pallas_call(
        functools.partial(kernel, n, own, s_lo, a_lo),
        out_shape=jax.ShapeDtypeStruct((channels, tokens), bf16),
        in_specs=[anywhere, anywhere, anywhere, vmem, anywhere, anywhere, anywhere, anywhere, vmem, vmem],
        out_specs=vmem,
        scratch_shapes=[
            pltpu.VMEM(filter_spectra.shape, bf16),
            pltpu.VMEM(projections.shape, bf16),
            pltpu.VMEM(short_filter.shape, f32),
            pltpu.VMEM(small.shape, bf16),
            pltpu.VMEM(twiddle.shape, f32),
            pltpu.VMEM(first.shape, bf16),
            pltpu.VMEM(last.shape, bf16),
            pltpu.VMEM((n, own * cols, SIDE), bf16),
            pltpu.VMEM((n, own * cols, SIDE), bf16),
            pltpu.VMEM((n, own * s_lo, SIDE), bf16),
            pltpu.VMEM((n, own * s_lo, SIDE), bf16),
            pltpu.VMEM((groups, n * GROUP * s_lo, SIDE), bf16),
            pltpu.VMEM((groups, n * GROUP * s_lo, SIDE), bf16),
            pltpu.VMEM((own // 2, 2 * SIDE, 2 * SIDE), bf16),
            pltpu.VMEM((SIDE, GROUP * 2 * SIDE), bf16),
            pltpu.VMEM((n, own, tokens), f32),
            pltpu.VMEM((channels, tokens), f32),
            pltpu.VMEM((channels, tokens), f32),
            pltpu.VMEM((16, channels), bf16),
            pltpu.VMEM((16, channels), bf16),
            dma((7,)),
            dma((2 + groups,)),
            dma((groups,)),
            dma((groups,)),
            dma,
            dma,
            dma((groups,)),
            dma((groups,)),
            dma,
            dma,
        ],
        compiler_params=pltpu.CompilerParams(collective_id=0, has_side_effects=True, vmem_limit_bytes=52 << 20),
        cost_estimate=pl.CostEstimate(flops=6_000_000_000, bytes_accessed=12_000_000, transcendentals=0),
    )(
        filter_spectra, projections, short_filter, skip_gain.reshape(channels // SIDE, SIDE),
        small, twiddle, first, last, tail, edge,
    )


def solution(mesh):
    return jax.shard_map(
        shards,
        mesh=mesh,
        in_specs=(P(None, "ch", "ctx"), P(None, "ch", None), P("ch"), P(None, "ch", "ctx")),
        out_specs=P("ch", "ctx"),
        check_vma=False,
    )
```

```python
import functools

import jax
import jax.numpy as jnp
import ml_dtypes
import numpy as np
from jax import lax
from jax.experimental import pallas as pl
from jax.experimental.pallas import tpu as pltpu
from jax.sharding import PartitionSpec as P

MESH = pl.DeviceIdType.MESH
SIDE = 128
GROUP = 8
AHEAD = 6
f32, bf16 = jnp.float32, jnp.bfloat16


def tables(n, own, s_lo, a_lo):
    period = SIDE * SIDE
    cols = 2 * a_lo
    wide = SIDE * s_lo
    order_f = np.zeros((own * cols, own * cols))
    c, j = np.meshgrid(np.arange(own), np.arange(cols), indexing="ij")
    order_f[(c * cols + j).ravel(), (j * own + c).ravel()] = 1
    order_x = np.zeros((wide, wide))
    c, s = np.meshgrid(np.arange(SIDE), np.arange(s_lo), indexing="ij")
    order_x[(c * s_lo + s).ravel(), (s * SIDE + c).ravel()] = 1
    order_y = np.zeros((wide, wide))
    q, c, s = np.meshgrid(np.arange(SIDE // GROUP), np.arange(GROUP), np.arange(s_lo), indexing="ij")
    order_y[(s * SIDE + q * GROUP + c).ravel(), ((q * GROUP + c) * s_lo + s).ravel()] = 1
    q, part, al = (v.ravel() for v in np.meshgrid(np.arange(n), np.arange(2), np.arange(a_lo), indexing="ij"))
    angle = 2 * np.pi * ((q * a_lo + al)[:, None] * np.arange(SIDE)[None, :] % SIDE) / SIDE
    wr, wi = np.cos(angle), -np.sin(angle)
    sign = np.where(part == 1, -1.0, 1.0)[:, None]
    forward = np.concatenate([np.concatenate([wr, -wi], 1), np.concatenate([wi, wr], 1) * sign], 0)
    vr, vi = np.cos(angle).T, np.sin(angle).T
    real = (part == 0)[None, :]
    inverse = np.concatenate([np.where(real, vr, -vi), np.where(real, vi, vr)], 0)
    tail = np.zeros((3, 16, wide))
    edge = np.zeros((3, 16, 2 * SIDE))
    for e in range(3):
        tail[e, 2 * e, wide - 2] = 1
        tail[e, 2 * e + 1, wide - 1] = 1
        edge[e, 2 * e + 1, 0] = 1
        edge[e, 2 * e, SIDE] = 1
        edge[e, 2 * e + 1, SIDE + 1] = 1
    shifts = [np.eye(wide, k=by) for by in (1, 2)]
    small = np.concatenate(
        [order_f, order_x, order_y, forward, inverse, *shifts, tail.reshape(48, -1), edge.reshape(48, -1)], 0
    )
    some = GROUP // 2
    s = np.arange(n * s_lo)
    angle = 2 * np.pi * (s[:, None] * np.arange(SIDE)[None, :] % SIDE) / SIDE
    first = np.zeros((n, some, s_lo, some, 2, SIDE))
    for g in range(some):
        first[:, g, :, g, 0] = np.cos(angle).reshape(n, s_lo, SIDE)
        first[:, g, :, g, 1] = -np.sin(angle).reshape(n, s_lo, SIDE)
    first = first.reshape(n * some * s_lo, some * 2 * SIDE)
    last = first / period
    angle = 2 * np.pi * np.arange(SIDE)[:, None] * np.arange(SIDE)[None, :] / period
    twiddle = np.concatenate([np.cos(angle), np.sin(angle)], 0)
    return [
        small.astype(ml_dtypes.bfloat16),
        twiddle.astype(np.float32),
        first.astype(ml_dtypes.bfloat16),
        last.astype(ml_dtypes.bfloat16),
    ]


def peer(me, o):
    z, x, c = me // 8, (me // 2) % 4, me % 2
    return (z + o // 8) % 4 * 8 + (x + o // 2) % 4 * 2 + (c + o) % 2


def dot(a, b):
    return jnp.dot(a, b, preferred_element_type=f32)


def dot_nt(a, b):
    return lax.dot_general(a, b, (((1,), (1,)), ((), ())), preferred_element_type=f32)


def dot_tn(a, b):
    return lax.dot_general(a, b, (((0,), (0,)), ((), ())), preferred_element_type=f32)


def kernel(
    n, own, s_lo, a_lo, chunks,
    filt_hbm, proj_hbm, taps_hbm, skip_hbm, small_hbm, twiddle_hbm, first_hbm, last_hbm,
    out,
    filt, proj, taps, skip, small, twiddle, first, last,
    fsend, fbuf, xsend, xbuf, ysend, ybuf, turned, spec, values, back, conv, query, direct, halo_out, halo_in,
    load_sem, own_sem, fsend_sem, frecv_sem, xsend_sem, xrecv_sem, ysend_sem, yrecv_sem, hsend_sem, hrecv_sem,
):
    me = lax.axis_index("ctx")
    groups = own // GROUP
    cols = 2 * a_lo
    some = GROUP // 2
    xrows = GROUP * s_lo
    blocks = n * own // SIDE
    per_block = SIDE // own
    half = n * cols
    wide = SIDE * s_lo

    barrier = pltpu.get_barrier_semaphore()

    def greet(i, carry):
        pl.semaphore_signal(barrier, inc=1, device_id={"ctx": peer(me, i)}, device_id_type=MESH)
        return carry

    lax.fori_loop(1, n, greet, 0)

    loads = [
        pltpu.make_async_copy(src, dst, load_sem.at[i])
        for i, (src, dst) in enumerate(
            [(small_hbm, small), (filt_hbm, filt), (proj_hbm, proj), (taps_hbm, taps), (skip_hbm, skip), (twiddle_hbm, twiddle), (first_hbm, first), (last_hbm, last)]
        )
    ]
    for load in loads:
        load.start()

    order_f = small.at[pl.ds(0, 256)]
    order_x = small.at[pl.ds(256, 256)]
    order_y = small.at[pl.ds(512, 256)]
    forward = small.at[pl.ds(768, 512)]
    inverse = small.at[pl.ds(1280, 256)]
    shifts = [small.at[pl.ds(1536, 256)], small.at[pl.ds(1792, 256)]]
    tails = [small.at[pl.ds(2048 + 16 * e, 16)] for e in range(3)]
    edges = [small.at[pl.ds(2096 + 16 * e, 16)] for e in range(3)]

    def at_peer(i):
        return peer(me, i * 11 % n)

    def arrange(i):
        owners = at_peer(2 * i), at_peer(2 * i + 1)
        sides = []
        for d in owners:
            rows = pl.ds(pl.multiple_of(d * own, own), own)
            sides.append([filt[part, rows, al * SIDE : (al + 1) * SIDE] for part in range(2) for al in range(a_lo)])
        stacked = jnp.concatenate([jnp.concatenate(side, axis=0) for side in sides], axis=1)
        arranged = dot(order_f[...], stacked).astype(bf16)
        for k, d in enumerate(owners):
            fsend[d] = arranged[:, k * SIDE : (k + 1) * SIDE]

    def f_rows(chunk):
        start, count = chunks[chunk]
        return pl.ds(start * 2 * cols, count * 2 * cols)

    def f_send(chunk, i):
        rows = f_rows(chunk)
        d = at_peer(i)
        pltpu.make_async_remote_copy(
            src_ref=fsend.at[d, rows], dst_ref=fbuf.at[me, rows], send_sem=fsend_sem.at[chunk], recv_sem=frecv_sem.at[chunk],
            device_id={"ctx": d}, device_id_type=MESH,
        ).start()

    def f_all(chunk):
        rows = f_rows(chunk)
        return pltpu.make_async_remote_copy(
            src_ref=fsend.at[pl.ds(0, n - 1), rows], dst_ref=fbuf.at[pl.ds(0, n - 1), rows],
            send_sem=fsend_sem.at[chunk], recv_sem=frecv_sem.at[chunk],
            device_id={"ctx": (me + 1) % n}, device_id_type=MESH,
        )

    loads[0].wait()
    loads[1].wait()

    def ahead(i, carry):
        arrange(i)
        return carry

    lax.fori_loop(0, AHEAD, ahead, 0)
    own_f = pltpu.make_async_copy(fsend.at[me], fbuf.at[me], own_sem.at[0])
    own_f.start()

    loads[2].wait()
    halo_out[...] = sum(dot_nt(tails[e][...], proj[e]) for e in range(3)).astype(bf16)

    pl.semaphore_wait(barrier, n - 1)

    halo = pltpu.make_async_remote_copy(
        src_ref=halo_out, dst_ref=halo_in, send_sem=hsend_sem, recv_sem=hrecv_sem,
        device_id={"ctx": (me + 1) % n}, device_id_type=MESH,
    )
    halo.start()

    def send_ready(i, carry):
        f_send(0, i)
        return carry

    lax.fori_loop(1, 2 * AHEAD, send_ready, 0)

    def arrange_send(i, carry):
        arrange(i)
        f_send(0, 2 * i)
        f_send(0, 2 * i + 1)
        return carry

    lax.fori_loop(AHEAD, n // 2, arrange_send, 0)

    loads[3].wait()
    loads[4].wait()
    halo.wait_recv()
    inside = jnp.where(me == 0, 0.0, 1.0).astype(f32)

    def gate(blk, carry):
        rows = pl.ds(pl.multiple_of(blk * SIDE, SIDE), SIDE)
        halo_rows = halo_in[:, rows]
        columns = jnp.concatenate(
            [taps[e, :, rows] for e in range(3)] + [skip[pl.ds(blk, 1), :], jnp.zeros((SIDE - 10, SIDE), f32)], axis=0
        ).T
        filtered = []
        for e in range(3):
            x = proj[e, rows, :]
            before = dot_tn(halo_rows, edges[e][...]) * inside
            back1, back2 = dot(x, shifts[0][...]), dot(x, shifts[1][...])
            back1 = jnp.concatenate([back1[:, :SIDE] + before[:, :SIDE], back1[:, SIDE:]], axis=1)
            back2 = jnp.concatenate([back2[:, :SIDE] + before[:, SIDE:], back2[:, SIDE:]], axis=1)
            tap = columns[:, 3 * e : 3 * e + 3]
            filtered.append(tap[:, 0:1] * x.astype(f32) + tap[:, 1:2] * back1 + tap[:, 2:3] * back2)
        product = (filtered[1] * filtered[2]).astype(bf16)
        owners = pl.ds(pl.multiple_of(blk * per_block, per_block), per_block)
        query[owners] = filtered[0].reshape(per_block, own, wide)
        direct[owners] = (columns[:, 9:10] * product.astype(f32)).reshape(per_block, own, wide)
        stacked = jnp.concatenate([product[:, s * SIDE : (s + 1) * SIDE] for s in range(s_lo)], axis=0)
        xsend[owners] = dot(order_x[...], stacked).astype(bf16).reshape(per_block, own * s_lo, SIDE)
        return carry

    lax.fori_loop(0, blocks, gate, 0)

    x_all = pltpu.make_async_remote_copy(
        src_ref=xsend.at[pl.ds(0, n - 1)], dst_ref=xbuf.at[pl.ds(0, n - 1)], send_sem=xsend_sem, recv_sem=xrecv_sem,
        device_id={"ctx": (me + 1) % n}, device_id_type=MESH,
    )

    def x_start(i, carry):
        d = at_peer(i)
        pltpu.make_async_remote_copy(
            src_ref=xsend.at[d], dst_ref=xbuf.at[me], send_sem=xsend_sem, recv_sem=xrecv_sem,
            device_id={"ctx": d}, device_id_type=MESH,
        ).start()
        return carry

    lax.fori_loop(1, n, x_start, 0)
    own_x = pltpu.make_async_copy(xsend.at[me], xbuf.at[me], own_sem.at[1])
    own_x.start()

    for chunk in range(1, len(chunks)):

        def f_start(i, carry, chunk=chunk):
            f_send(chunk, i)
            return carry

        lax.fori_loop(1, n, f_start, 0)

    for load in loads[5:]:
        load.wait()
    own_x.wait()
    x_all.wait_recv()
    cos, sin = twiddle[0:SIDE, :], twiddle[SIDE : 2 * SIDE, :]

    for g in range(groups):
        taken = xbuf[:, g * xrows : (g + 1) * xrows, :].astype(f32)
        for k in range(2):
            block = taken[:, k * some * s_lo : (k + 1) * some * s_lo, :].reshape(n * some * s_lo, SIDE)
            turned[(2 * g + k) * SIDE : (2 * g + k + 1) * SIDE, :] = block.T.astype(bf16)

    def over_s(g, carry):
        rows = pl.ds(pl.multiple_of(g * 2 * SIDE, 2 * SIDE), 2 * SIDE)
        for c in range(some):
            part = dot(turned[rows, :], first[:, c * 2 * SIDE : (c + 1) * 2 * SIDE])
            lanes = slice(c % 2 * SIDE, (c % 2 + 1) * SIDE)
            for k in range(2):
                re, im = part[k * SIDE : (k + 1) * SIDE, :SIDE], part[k * SIDE : (k + 1) * SIDE, SIDE:]
                pair = g * some + k * 2 + c // 2
                spec[pair, 0:SIDE, lanes] = (re * cos + im * sin).astype(bf16)
                spec[pair, SIDE : 2 * SIDE, lanes] = (im * cos - re * sin).astype(bf16)
        return carry

    lax.fori_loop(0, groups, over_s, 0)

    def over_r(i, carry):
        for k in range(2):
            values[2 * i + k] = dot(forward[...], spec[2 * i + k])
        return carry

    lax.fori_loop(0, own // 4, over_r, 0)

    own_f.wait()

    def through(h, k):
        for j in range(2):
            pair = 2 * h + j
            taken = fbuf[:, pl.ds(pl.multiple_of(pair * 2 * cols, 2 * cols), 2 * cols), :].astype(f32)
            shaped = []
            for c in range(2):
                gains = taken[:, c * cols : (c + 1) * cols, :]
                lanes = slice(c * SIDE, (c + 1) * SIDE)
                straight = values[pair, 0:half, lanes].reshape(n, cols, SIDE) * gains
                crossed = values[pair, half : 2 * half, lanes].reshape(n, cols, SIDE) * gains
                shaped.append((straight + pltpu.roll(crossed, a_lo, 1)).reshape(half, SIDE).astype(bf16))
            part = dot(inverse[...], jnp.concatenate(shaped, axis=1))
            rows = pl.ds(pl.multiple_of(k * SIDE, SIDE), SIDE)
            for c in range(2):
                re, im = part[:SIDE, c * SIDE : (c + 1) * SIDE], part[SIDE:, c * SIDE : (c + 1) * SIDE]
                at = (2 * j + c) * 2 * SIDE
                back[rows, at : at + SIDE] = (re * cos - im * sin).astype(bf16)
                back[rows, at + SIDE : at + 2 * SIDE] = (re * sin + im * cos).astype(bf16)

    def y_all(g):
        return pltpu.make_async_remote_copy(
            src_ref=ysend.at[g, pl.ds(0, (n - 1) * xrows)], dst_ref=ybuf.at[g, pl.ds(0, (n - 1) * xrows)],
            send_sem=ysend_sem.at[g], recv_sem=yrecv_sem.at[g], device_id={"ctx": (me + 1) % n}, device_id_type=MESH,
        )

    arrives = {start: chunk for chunk, (start, _) in enumerate(chunks)}
    own_y = []
    for g in range(groups):
        pairs = range(some * g, some * g + some)
        if pairs[0] in arrives:
            f_all(arrives[pairs[0]]).wait_recv()
        if pairs[2] in arrives:
            through(2 * g, 0)
            f_all(arrives[pairs[2]]).wait_recv()
            through(2 * g + 1, 1)
        else:

            def both(k, carry, g=g):
                through(2 * g + k, k)
                return carry

            lax.fori_loop(0, 2, both, 0)
        part = dot_nt(last[...], back[...])
        part = jnp.concatenate([part[:, k * SIDE : (k + 1) * SIDE].reshape(n, some * s_lo, SIDE) for k in range(2)], axis=1)
        ysend[g] = part.reshape(n * xrows, SIDE).astype(bf16)

        def y_start(i, carry, g=g):
            d = at_peer(i)
            pltpu.make_async_remote_copy(
                src_ref=ysend.at[g, pl.ds(pl.multiple_of(d * xrows, xrows), xrows)],
                dst_ref=ybuf.at[g, pl.ds(pl.multiple_of(me * xrows, xrows), xrows)],
                send_sem=ysend_sem.at[g], recv_sem=yrecv_sem.at[g], device_id={"ctx": d}, device_id_type=MESH,
            ).start()
            return carry

        lax.fori_loop(1, n, y_start, 0)
        mine = pl.ds(pl.multiple_of(me * xrows, xrows), xrows)
        own_y.append(pltpu.make_async_copy(ysend.at[g, mine], ybuf.at[g, mine], own_sem.at[2 + g]))
        own_y[g].start()

    owners = SIDE // GROUP
    for g in range(groups):
        own_y[g].wait()
        y_all(g).wait_recv()
        count = n // owners
        stacked = [ybuf[g, h * owners * xrows : (h + 1) * owners * xrows, :] for h in range(count)]
        arranged = dot(order_y[...], jnp.concatenate(stacked, axis=1))
        for h in range(count):
            for s in range(s_lo):
                conv[h * owners : (h + 1) * owners, g * GROUP : (g + 1) * GROUP, s * SIDE : (s + 1) * SIDE] = arranged[
                    s * SIDE : (s + 1) * SIDE, h * SIDE : (h + 1) * SIDE
                ].reshape(owners, GROUP, SIDE)
        if g % 2 == 1:
            rows = slice((g - 1) * GROUP, (g + 1) * GROUP)
            out[:, rows, :] = (query[:, rows, :] * (conv[:, rows, :] + direct[:, rows, :])).astype(bf16)

    halo.wait_send()
    x_all.wait_send()
    for chunk in range(len(chunks)):
        f_all(chunk).wait_send()
    for g in range(groups):
        y_all(g).wait_send()


def shards(projections, short_filter, skip_gain, filter_spectra):
    n = lax.axis_size("ctx")
    channels, tokens = projections.shape[1:]
    freqs = filter_spectra.shape[2]
    own, s_lo, a_lo = channels // n, tokens // SIDE, freqs // SIDE
    groups = own // GROUP
    cols = 2 * a_lo
    pairs = own // 2
    chunks = [(0, pairs // 2), (pairs // 2, pairs // 4), (pairs * 3 // 4, pairs // 8), (pairs * 7 // 8, pairs // 8)]
    hbm, vmem = pl.BlockSpec(memory_space=pltpu.HBM), pl.BlockSpec(memory_space=pltpu.VMEM)
    small, twiddle, first, last = tables(n, own, s_lo, a_lo)
    dma = pltpu.SemaphoreType.DMA
    return pl.pallas_call(
        functools.partial(kernel, n, own, s_lo, a_lo, chunks),
        out_shape=jax.ShapeDtypeStruct((n, own, tokens), bf16),
        in_specs=[hbm] * 8,
        out_specs=vmem,
        scratch_shapes=[
            pltpu.VMEM(filter_spectra.shape, bf16),
            pltpu.VMEM(projections.shape, bf16),
            pltpu.VMEM((3, 3, channels), f32),
            pltpu.VMEM((channels // SIDE, SIDE), f32),
            pltpu.VMEM(small.shape, bf16),
            pltpu.VMEM(twiddle.shape, f32),
            pltpu.VMEM(first.shape, bf16),
            pltpu.VMEM(last.shape, bf16),
            pltpu.VMEM((n, own * cols, SIDE), bf16),
            pltpu.VMEM((n, own * cols, SIDE), bf16),
            pltpu.VMEM((n, own * s_lo, SIDE), bf16),
            pltpu.VMEM((n, own * s_lo, SIDE), bf16),
            pltpu.VMEM((groups, n * GROUP * s_lo, SIDE), bf16),
            pltpu.VMEM((groups, n * GROUP * s_lo, SIDE), bf16),
            pltpu.VMEM((2 * groups * SIDE, n * GROUP * s_lo // 2), bf16),
            pltpu.VMEM((own // 2, 2 * SIDE, 2 * SIDE), bf16),
            pltpu.VMEM((own // 2, 4 * SIDE, 2 * SIDE), f32),
            pltpu.VMEM((2 * SIDE, GROUP * SIDE), bf16),
            pltpu.VMEM((n, own, tokens), f32),
            pltpu.VMEM((n, own, tokens), f32),
            pltpu.VMEM((n, own, tokens), f32),
            pltpu.VMEM((16, channels), bf16),
            pltpu.VMEM((16, channels), bf16),
            dma((8,)),
            dma((2 + groups,)),
            dma((len(chunks),)),
            dma((len(chunks),)),
            dma,
            dma,
            dma((groups,)),
            dma((groups,)),
            dma,
            dma,
        ],
        compiler_params=pltpu.CompilerParams(collective_id=0, has_side_effects=True, vmem_limit_bytes=62 << 20),
        cost_estimate=pl.CostEstimate(flops=6_000_000_000, bytes_accessed=12_000_000, transcendentals=0),
    )(
        filter_spectra, projections, jnp.swapaxes(short_filter, 1, 2), skip_gain.reshape(channels // SIDE, SIDE),
        small, twiddle, first, last,
    ).reshape(channels, tokens)


def solution(mesh):
    return jax.shard_map(
        shards,
        mesh=mesh,
        in_specs=(P(None, "ch", "ctx"), P(None, "ch", None), P("ch"), P(None, "ch", "ctx")),
        out_specs=P("ch", "ctx"),
        check_vma=False,
    )
```

```python
import functools

import jax
import jax.numpy as jnp
import ml_dtypes
import numpy as np
from jax import lax
from jax.experimental import pallas as pl
from jax.experimental.pallas import tpu as pltpu
from jax.sharding import PartitionSpec as P

MESH = pl.DeviceIdType.MESH
SIDE = 128
GROUP = 8
AHEAD = 6
f32, bf16 = jnp.float32, jnp.bfloat16


def tables(n, own, s_lo, a_lo):
    period = SIDE * SIDE
    cols = 2 * a_lo
    wide = SIDE * s_lo
    order_f = np.zeros((own * cols, own * cols))
    c, j = np.meshgrid(np.arange(own), np.arange(cols), indexing="ij")
    order_f[(c * cols + j).ravel(), (j * own + c).ravel()] = 1
    order_x = np.zeros((wide, wide))
    c, s = np.meshgrid(np.arange(SIDE), np.arange(s_lo), indexing="ij")
    order_x[(c * s_lo + s).ravel(), (s * SIDE + c).ravel()] = 1
    order_y = np.zeros((wide, wide))
    q, c, s = np.meshgrid(np.arange(SIDE // GROUP), np.arange(GROUP), np.arange(s_lo), indexing="ij")
    order_y[(s * SIDE + q * GROUP + c).ravel(), ((q * GROUP + c) * s_lo + s).ravel()] = 1
    q, part, al = (v.ravel() for v in np.meshgrid(np.arange(n), np.arange(2), np.arange(a_lo), indexing="ij"))
    angle = 2 * np.pi * ((q * a_lo + al)[:, None] * np.arange(SIDE)[None, :] % SIDE) / SIDE
    wr, wi = np.cos(angle), -np.sin(angle)
    sign = np.where(part == 1, -1.0, 1.0)[:, None]
    forward = np.concatenate([np.concatenate([wr, -wi], 1), np.concatenate([wi, wr], 1) * sign], 0)
    vr, vi = np.cos(angle).T, np.sin(angle).T
    real = (part == 0)[None, :]
    inverse = np.concatenate([np.where(real, vr, -vi), np.where(real, vi, vr)], 0)
    tail = np.zeros((3, 16, wide))
    edge = np.zeros((3, 16, 2 * SIDE))
    for e in range(3):
        tail[e, 2 * e, wide - 2] = 1
        tail[e, 2 * e + 1, wide - 1] = 1
        edge[e, 2 * e + 1, 0] = 1
        edge[e, 2 * e, SIDE] = 1
        edge[e, 2 * e + 1, SIDE + 1] = 1
    shifts = [np.eye(wide, k=by) for by in (1, 2)]
    small = np.concatenate(
        [order_f, order_x, order_y, forward, inverse, *shifts, tail.reshape(48, -1), edge.reshape(48, -1)], 0
    )
    some = GROUP // 2
    s = np.arange(n * s_lo)
    angle = 2 * np.pi * (s[:, None] * np.arange(SIDE)[None, :] % SIDE) / SIDE
    first = np.zeros((n, some, s_lo, some, 2, SIDE))
    for g in range(some):
        first[:, g, :, g, 0] = np.cos(angle).reshape(n, s_lo, SIDE)
        first[:, g, :, g, 1] = -np.sin(angle).reshape(n, s_lo, SIDE)
    first = first.reshape(n * some * s_lo, some * 2 * SIDE)
    last = first / period
    angle = 2 * np.pi * np.arange(SIDE)[:, None] * np.arange(SIDE)[None, :] / period
    twiddle = np.concatenate([np.cos(angle), np.sin(angle)], 0)
    return [
        small.astype(ml_dtypes.bfloat16),
        twiddle.astype(np.float32),
        first.astype(ml_dtypes.bfloat16),
        last.astype(ml_dtypes.bfloat16),
    ]


def dot(a, b):
    return jnp.dot(a, b, preferred_element_type=f32)


def dot_nt(a, b):
    return lax.dot_general(a, b, (((1,), (1,)), ((), ())), preferred_element_type=f32)


def dot_tn(a, b):
    return lax.dot_general(a, b, (((0,), (0,)), ((), ())), preferred_element_type=f32)


def kernel(
    n, own, s_lo, a_lo, chunks,
    filt_hbm, proj_hbm, taps_hbm, skip_hbm, small_hbm, twiddle_hbm, first_hbm, last_hbm,
    out,
    filt, proj, taps, skip, small, twiddle, first, last,
    fsend, fbuf, xsend, xbuf, ysend, ybuf, turned, spec, values, back, conv, query, direct, halo_out, halo_in,
    load_sem, own_sem, fsend_sem, frecv_sem, xsend_sem, xrecv_sem, ysend_sem, yrecv_sem, hsend_sem, hrecv_sem,
):
    me = lax.axis_index("ctx")
    groups = own // GROUP
    cols = 2 * a_lo
    some = GROUP // 2
    xrows = GROUP * s_lo
    blocks = n * own // SIDE
    per_block = SIDE // own
    half = n * cols
    wide = SIDE * s_lo

    barrier = pltpu.get_barrier_semaphore()

    def greet(i, carry):
        pl.semaphore_signal(barrier, inc=1, device_id={"ctx": lax.rem(me + i, n)}, device_id_type=MESH)
        return carry

    lax.fori_loop(1, n, greet, 0, unroll=True)

    loads = [
        pltpu.make_async_copy(src, dst, load_sem.at[i])
        for i, (src, dst) in enumerate(
            [(small_hbm, small), (filt_hbm, filt), (proj_hbm, proj), (taps_hbm, taps), (skip_hbm, skip), (twiddle_hbm, twiddle), (first_hbm, first), (last_hbm, last)]
        )
    ]
    for load in loads:
        load.start()

    order_f = small.at[pl.ds(0, 256)]
    order_x = small.at[pl.ds(256, 256)]
    order_y = small.at[pl.ds(512, 256)]
    forward = small.at[pl.ds(768, 512)]
    inverse = small.at[pl.ds(1280, 256)]
    shifts = [small.at[pl.ds(1536, 256)], small.at[pl.ds(1792, 256)]]
    tails = [small.at[pl.ds(2048 + 16 * e, 16)] for e in range(3)]
    edges = [small.at[pl.ds(2096 + 16 * e, 16)] for e in range(3)]

    def at_peer(i):
        return lax.rem(me + i * 5, n)

    def arrange(i):
        owners = at_peer(2 * i), at_peer(2 * i + 1)
        sides = []
        for d in owners:
            rows = pl.ds(pl.multiple_of(d * own, own), own)
            sides.append([filt[part, rows, al * SIDE : (al + 1) * SIDE] for part in range(2) for al in range(a_lo)])
        stacked = jnp.concatenate([jnp.concatenate(side, axis=0) for side in sides], axis=1)
        arranged = dot(order_f[...], stacked).astype(bf16)
        for k, d in enumerate(owners):
            fsend[d] = arranged[:, k * SIDE : (k + 1) * SIDE]

    def f_rows(chunk):
        start, count = chunks[chunk]
        return pl.ds(start * 2 * cols, count * 2 * cols)

    def f_send(chunk, i):
        rows = f_rows(chunk)
        d = at_peer(i)
        pltpu.make_async_remote_copy(
            src_ref=fsend.at[d, rows], dst_ref=fbuf.at[me, rows], send_sem=fsend_sem.at[chunk], recv_sem=frecv_sem.at[chunk],
            device_id={"ctx": d}, device_id_type=MESH,
        ).start()

    def f_all(chunk):
        rows = f_rows(chunk)
        return pltpu.make_async_remote_copy(
            src_ref=fsend.at[pl.ds(0, n - 1), rows], dst_ref=fbuf.at[pl.ds(0, n - 1), rows],
            send_sem=fsend_sem.at[chunk], recv_sem=frecv_sem.at[chunk],
            device_id={"ctx": (me + 1) % n}, device_id_type=MESH,
        )

    loads[0].wait()
    loads[1].wait()

    def ahead(i, carry):
        arrange(i)
        return carry

    lax.fori_loop(0, AHEAD, ahead, 0)
    own_f = pltpu.make_async_copy(fsend.at[me], fbuf.at[me], own_sem.at[0])
    own_f.start()

    loads[2].wait()
    halo_out[...] = sum(dot_nt(tails[e][...], proj[e]) for e in range(3)).astype(bf16)

    pl.semaphore_wait(barrier, n - 1)

    halo = pltpu.make_async_remote_copy(
        src_ref=halo_out, dst_ref=halo_in, send_sem=hsend_sem, recv_sem=hrecv_sem,
        device_id={"ctx": (me + 1) % n}, device_id_type=MESH,
    )
    halo.start()

    def send_ready(i, carry):
        f_send(0, i)
        return carry

    lax.fori_loop(1, 2 * AHEAD, send_ready, 0)

    def arrange_send(i, carry):
        arrange(i)
        f_send(0, 2 * i)
        f_send(0, 2 * i + 1)
        return carry

    lax.fori_loop(AHEAD, n // 2, arrange_send, 0)

    loads[3].wait()
    loads[4].wait()
    halo.wait_recv()
    inside = jnp.where(me == 0, 0.0, 1.0).astype(f32)

    def gate(blk, carry):
        rows = pl.ds(pl.multiple_of(blk * SIDE, SIDE), SIDE)
        halo_rows = halo_in[:, rows]
        columns = jnp.concatenate(
            [taps[e, :, rows] for e in range(3)] + [skip[pl.ds(blk, 1), :], jnp.zeros((SIDE - 10, SIDE), f32)], axis=0
        ).T
        filtered = []
        for e in range(3):
            x = proj[e, rows, :]
            before = dot_tn(halo_rows, edges[e][...]) * inside
            back1, back2 = dot(x, shifts[0][...]), dot(x, shifts[1][...])
            back1 = jnp.concatenate([back1[:, :SIDE] + before[:, :SIDE], back1[:, SIDE:]], axis=1)
            back2 = jnp.concatenate([back2[:, :SIDE] + before[:, SIDE:], back2[:, SIDE:]], axis=1)
            tap = columns[:, 3 * e : 3 * e + 3]
            filtered.append(tap[:, 0:1] * x.astype(f32) + tap[:, 1:2] * back1 + tap[:, 2:3] * back2)
        product = (filtered[1] * filtered[2]).astype(bf16)
        owners = pl.ds(pl.multiple_of(blk * per_block, per_block), per_block)
        query[owners] = filtered[0].reshape(per_block, own, wide)
        direct[owners] = (columns[:, 9:10] * product.astype(f32)).reshape(per_block, own, wide)
        stacked = jnp.concatenate([product[:, s * SIDE : (s + 1) * SIDE] for s in range(s_lo)], axis=0)
        xsend[owners] = dot(order_x[...], stacked).astype(bf16).reshape(per_block, own * s_lo, SIDE)
        return carry

    lax.fori_loop(0, blocks, gate, 0)

    x_all = pltpu.make_async_remote_copy(
        src_ref=xsend.at[pl.ds(0, n - 1)], dst_ref=xbuf.at[pl.ds(0, n - 1)], send_sem=xsend_sem, recv_sem=xrecv_sem,
        device_id={"ctx": (me + 1) % n}, device_id_type=MESH,
    )

    def x_start(i, carry):
        d = at_peer(i)
        pltpu.make_async_remote_copy(
            src_ref=xsend.at[d], dst_ref=xbuf.at[me], send_sem=xsend_sem, recv_sem=xrecv_sem,
            device_id={"ctx": d}, device_id_type=MESH,
        ).start()
        return carry

    lax.fori_loop(1, n, x_start, 0)
    own_x = pltpu.make_async_copy(xsend.at[me], xbuf.at[me], own_sem.at[1])
    own_x.start()

    for chunk in range(1, len(chunks)):

        def f_start(i, carry, chunk=chunk):
            f_send(chunk, i)
            return carry

        lax.fori_loop(1, n, f_start, 0)

    for load in loads[5:]:
        load.wait()
    own_x.wait()
    x_all.wait_recv()
    cos, sin = twiddle[0:SIDE, :], twiddle[SIDE : 2 * SIDE, :]

    for g in range(groups):
        taken = xbuf[:, g * xrows : (g + 1) * xrows, :].astype(f32)
        for k in range(2):
            block = taken[:, k * some * s_lo : (k + 1) * some * s_lo, :].reshape(n * some * s_lo, SIDE)
            turned[(2 * g + k) * SIDE : (2 * g + k + 1) * SIDE, :] = block.T.astype(bf16)

    def over_s(g, carry):
        rows = pl.ds(pl.multiple_of(g * 2 * SIDE, 2 * SIDE), 2 * SIDE)
        for c in range(some):
            part = dot(turned[rows, :], first[:, c * 2 * SIDE : (c + 1) * 2 * SIDE])
            lanes = slice(c % 2 * SIDE, (c % 2 + 1) * SIDE)
            for k in range(2):
                re, im = part[k * SIDE : (k + 1) * SIDE, :SIDE], part[k * SIDE : (k + 1) * SIDE, SIDE:]
                pair = g * some + k * 2 + c // 2
                spec[pair, 0:SIDE, lanes] = (re * cos + im * sin).astype(bf16)
                spec[pair, SIDE : 2 * SIDE, lanes] = (im * cos - re * sin).astype(bf16)
        return carry

    lax.fori_loop(0, groups, over_s, 0)

    def over_r(i, carry):
        for k in range(2):
            values[2 * i + k] = dot(forward[...], spec[2 * i + k])
        return carry

    lax.fori_loop(0, own // 4, over_r, 0)

    own_f.wait()

    def through(h, k):
        for j in range(2):
            pair = 2 * h + j
            taken = fbuf[:, pl.ds(pl.multiple_of(pair * 2 * cols, 2 * cols), 2 * cols), :].astype(f32)
            shaped = []
            for c in range(2):
                gains = taken[:, c * cols : (c + 1) * cols, :]
                lanes = slice(c * SIDE, (c + 1) * SIDE)
                straight = values[pair, 0:half, lanes].reshape(n, cols, SIDE) * gains
                crossed = values[pair, half : 2 * half, lanes].reshape(n, cols, SIDE) * gains
                shaped.append((straight + pltpu.roll(crossed, a_lo, 1)).reshape(half, SIDE).astype(bf16))
            part = dot(inverse[...], jnp.concatenate(shaped, axis=1))
            rows = pl.ds(pl.multiple_of(k * SIDE, SIDE), SIDE)
            for c in range(2):
                re, im = part[:SIDE, c * SIDE : (c + 1) * SIDE], part[SIDE:, c * SIDE : (c + 1) * SIDE]
                at = (2 * j + c) * 2 * SIDE
                back[rows, at : at + SIDE] = (re * cos - im * sin).astype(bf16)
                back[rows, at + SIDE : at + 2 * SIDE] = (re * sin + im * cos).astype(bf16)

    def y_all(g):
        return pltpu.make_async_remote_copy(
            src_ref=ysend.at[g, pl.ds(0, (n - 1) * xrows)], dst_ref=ybuf.at[g, pl.ds(0, (n - 1) * xrows)],
            send_sem=ysend_sem.at[g], recv_sem=yrecv_sem.at[g], device_id={"ctx": (me + 1) % n}, device_id_type=MESH,
        )

    arrives = {start: chunk for chunk, (start, _) in enumerate(chunks)}
    own_y = []
    for g in range(groups):
        pairs = range(some * g, some * g + some)
        if pairs[0] in arrives:
            f_all(arrives[pairs[0]]).wait_recv()
        if pairs[2] in arrives:
            through(2 * g, 0)
            f_all(arrives[pairs[2]]).wait_recv()
            through(2 * g + 1, 1)
        else:

            def both(k, carry, g=g):
                through(2 * g + k, k)
                return carry

            lax.fori_loop(0, 2, both, 0)
        part = dot_nt(last[...], back[...])
        part = jnp.concatenate([part[:, k * SIDE : (k + 1) * SIDE].reshape(n, some * s_lo, SIDE) for k in range(2)], axis=1)
        ysend[g] = part.reshape(n * xrows, SIDE).astype(bf16)

        def y_start(i, carry, g=g):
            d = at_peer(i)
            pltpu.make_async_remote_copy(
                src_ref=ysend.at[g, pl.ds(pl.multiple_of(d * xrows, xrows), xrows)],
                dst_ref=ybuf.at[g, pl.ds(pl.multiple_of(me * xrows, xrows), xrows)],
                send_sem=ysend_sem.at[g], recv_sem=yrecv_sem.at[g], device_id={"ctx": d}, device_id_type=MESH,
            ).start()
            return carry

        lax.fori_loop(1, n, y_start, 0)
        mine = pl.ds(pl.multiple_of(me * xrows, xrows), xrows)
        own_y.append(pltpu.make_async_copy(ysend.at[g, mine], ybuf.at[g, mine], own_sem.at[2 + g]))
        own_y[g].start()

    owners = SIDE // GROUP
    for g in range(groups):
        own_y[g].wait()
        y_all(g).wait_recv()
        count = n // owners
        stacked = [ybuf[g, h * owners * xrows : (h + 1) * owners * xrows, :] for h in range(count)]
        arranged = dot(order_y[...], jnp.concatenate(stacked, axis=1))
        for h in range(count):
            for s in range(s_lo):
                conv[h * owners : (h + 1) * owners, g * GROUP : (g + 1) * GROUP, s * SIDE : (s + 1) * SIDE] = arranged[
                    s * SIDE : (s + 1) * SIDE, h * SIDE : (h + 1) * SIDE
                ].reshape(owners, GROUP, SIDE)
        if g % 2 == 1:
            rows = slice((g - 1) * GROUP, (g + 1) * GROUP)
            out[:, rows, :] = (query[:, rows, :] * (conv[:, rows, :] + direct[:, rows, :])).astype(bf16)

    halo.wait_send()
    x_all.wait_send()
    for chunk in range(len(chunks)):
        f_all(chunk).wait_send()
    for g in range(groups):
        y_all(g).wait_send()


def shards(projections, short_filter, skip_gain, filter_spectra):
    n = lax.axis_size("ctx")
    channels, tokens = projections.shape[1:]
    freqs = filter_spectra.shape[2]
    own, s_lo, a_lo = channels // n, tokens // SIDE, freqs // SIDE
    groups = own // GROUP
    cols = 2 * a_lo
    pairs = own // 2
    chunks = [(0, pairs // 2), (pairs // 2, pairs // 4), (pairs * 3 // 4, pairs // 8), (pairs * 7 // 8, pairs // 8)]
    hbm, vmem = pl.BlockSpec(memory_space=pltpu.HBM), pl.BlockSpec(memory_space=pltpu.VMEM)
    small, twiddle, first, last = tables(n, own, s_lo, a_lo)
    dma = pltpu.SemaphoreType.DMA
    return pl.pallas_call(
        functools.partial(kernel, n, own, s_lo, a_lo, chunks),
        out_shape=jax.ShapeDtypeStruct((n, own, tokens), bf16),
        in_specs=[hbm] * 8,
        out_specs=vmem,
        scratch_shapes=[
            pltpu.VMEM(filter_spectra.shape, bf16),
            pltpu.VMEM(projections.shape, bf16),
            pltpu.VMEM((3, 3, channels), f32),
            pltpu.VMEM((channels // SIDE, SIDE), f32),
            pltpu.VMEM(small.shape, bf16),
            pltpu.VMEM(twiddle.shape, f32),
            pltpu.VMEM(first.shape, bf16),
            pltpu.VMEM(last.shape, bf16),
            pltpu.VMEM((n, own * cols, SIDE), bf16),
            pltpu.VMEM((n, own * cols, SIDE), bf16),
            pltpu.VMEM((n, own * s_lo, SIDE), bf16),
            pltpu.VMEM((n, own * s_lo, SIDE), bf16),
            pltpu.VMEM((groups, n * GROUP * s_lo, SIDE), bf16),
            pltpu.VMEM((groups, n * GROUP * s_lo, SIDE), bf16),
            pltpu.VMEM((2 * groups * SIDE, n * GROUP * s_lo // 2), bf16),
            pltpu.VMEM((own // 2, 2 * SIDE, 2 * SIDE), bf16),
            pltpu.VMEM((own // 2, 4 * SIDE, 2 * SIDE), f32),
            pltpu.VMEM((2 * SIDE, GROUP * SIDE), bf16),
            pltpu.VMEM((n, own, tokens), f32),
            pltpu.VMEM((n, own, tokens), f32),
            pltpu.VMEM((n, own, tokens), f32),
            pltpu.VMEM((16, channels), bf16),
            pltpu.VMEM((16, channels), bf16),
            dma((8,)),
            dma((2 + groups,)),
            dma((len(chunks),)),
            dma((len(chunks),)),
            dma,
            dma,
            dma((groups,)),
            dma((groups,)),
            dma,
            dma,
        ],
        compiler_params=pltpu.CompilerParams(collective_id=0, has_side_effects=True, vmem_limit_bytes=62 << 20),
        cost_estimate=pl.CostEstimate(flops=6_000_000_000, bytes_accessed=12_000_000, transcendentals=0),
    )(
        filter_spectra, projections, jnp.swapaxes(short_filter, 1, 2), skip_gain.reshape(channels // SIDE, SIDE),
        small, twiddle, first, last,
    ).reshape(channels, tokens)


def solution(mesh):
    return jax.shard_map(
        shards,
        mesh=mesh,
        in_specs=(P(None, "ch", "ctx"), P(None, "ch", None), P("ch"), P(None, "ch", "ctx")),
        out_specs=P("ch", "ctx"),
        check_vma=False,
    )
```

```python
import functools

import jax
import jax.numpy as jnp
import ml_dtypes
import numpy as np
from jax import lax
from jax.experimental import pallas as pl
from jax.experimental.pallas import tpu as pltpu
from jax.sharding import PartitionSpec as P

MESH = pl.DeviceIdType.MESH
SIDE = 128
GROUP = 8
AHEAD = 6
f32, bf16 = jnp.float32, jnp.bfloat16


def tables(n, own, s_lo, a_lo):
    period = SIDE * SIDE
    cols = 2 * a_lo
    wide = SIDE * s_lo
    order_f = np.zeros((own * cols, own * cols))
    c, j = np.meshgrid(np.arange(own), np.arange(cols), indexing="ij")
    order_f[(c * cols + j).ravel(), (j * own + c).ravel()] = 1
    order_x = np.zeros((wide, wide))
    c, s = np.meshgrid(np.arange(SIDE), np.arange(s_lo), indexing="ij")
    order_x[(c * s_lo + s).ravel(), (s * SIDE + c).ravel()] = 1
    order_y = np.zeros((wide, wide))
    q, c, s = np.meshgrid(np.arange(SIDE // GROUP), np.arange(GROUP), np.arange(s_lo), indexing="ij")
    order_y[(s * SIDE + q * GROUP + c).ravel(), ((q * GROUP + c) * s_lo + s).ravel()] = 1
    q, part, al = (v.ravel() for v in np.meshgrid(np.arange(n), np.arange(2), np.arange(a_lo), indexing="ij"))
    angle = 2 * np.pi * ((q * a_lo + al)[:, None] * np.arange(SIDE)[None, :] % SIDE) / SIDE
    wr, wi = np.cos(angle), -np.sin(angle)
    sign = np.where(part == 1, -1.0, 1.0)[:, None]
    forward = np.concatenate([np.concatenate([wr, -wi], 1), np.concatenate([wi, wr], 1) * sign], 0)
    vr, vi = np.cos(angle).T, np.sin(angle).T
    real = (part == 0)[None, :]
    inverse = np.concatenate([np.where(real, vr, -vi), np.where(real, vi, vr)], 0)
    tail = np.zeros((3, 16, wide))
    edge = np.zeros((3, 16, 2 * SIDE))
    for e in range(3):
        tail[e, 2 * e, wide - 2] = 1
        tail[e, 2 * e + 1, wide - 1] = 1
        edge[e, 2 * e + 1, 0] = 1
        edge[e, 2 * e, SIDE] = 1
        edge[e, 2 * e + 1, SIDE + 1] = 1
    shifts = [np.eye(wide, k=by) for by in (1, 2)]
    small = np.concatenate(
        [order_f, order_x, order_y, forward, inverse, *shifts, tail.reshape(48, -1), edge.reshape(48, -1)], 0
    )
    some = GROUP // 2
    s = np.arange(n * s_lo)
    angle = 2 * np.pi * (s[:, None] * np.arange(SIDE)[None, :] % SIDE) / SIDE
    first = np.zeros((n, some, s_lo, some, 2, SIDE))
    for g in range(some):
        first[:, g, :, g, 0] = np.cos(angle).reshape(n, s_lo, SIDE)
        first[:, g, :, g, 1] = -np.sin(angle).reshape(n, s_lo, SIDE)
    first = first.reshape(n * some * s_lo, some * 2 * SIDE)
    last = first / period
    angle = 2 * np.pi * np.arange(SIDE)[:, None] * np.arange(SIDE)[None, :] / period
    twiddle = np.concatenate([np.cos(angle), np.sin(angle)], 0)
    return [
        small.astype(ml_dtypes.bfloat16),
        twiddle.astype(np.float32),
        first.astype(ml_dtypes.bfloat16),
        last.astype(ml_dtypes.bfloat16),
    ]


def dot(a, b):
    return jnp.dot(a, b, preferred_element_type=f32)


def dot_nt(a, b):
    return lax.dot_general(a, b, (((1,), (1,)), ((), ())), preferred_element_type=f32)


def dot_tn(a, b):
    return lax.dot_general(a, b, (((0,), (0,)), ((), ())), preferred_element_type=f32)


def kernel(
    n, own, s_lo, a_lo, chunks,
    filt_hbm, proj_hbm, taps_hbm, skip_hbm, small_hbm, twiddle_hbm, first_hbm, last_hbm,
    out,
    filt, proj, taps, skip, small, twiddle, first, last,
    fsend, fbuf, xsend, xbuf, ysend, ybuf, turned, spec, values, back, conv, query, direct, halo_out, halo_in,
    load_sem, own_sem, fsend_sem, frecv_sem, xsend_sem, xrecv_sem, ysend_sem, yrecv_sem, hsend_sem, hrecv_sem,
):
    me = lax.axis_index("ctx")
    groups = own // GROUP
    cols = 2 * a_lo
    some = GROUP // 2
    xrows = GROUP * s_lo
    blocks = n * own // SIDE
    per_block = SIDE // own
    half = n * cols
    wide = SIDE * s_lo

    barrier = pltpu.get_barrier_semaphore()

    def greet(i, carry):
        pl.semaphore_signal(barrier, inc=1, device_id={"ctx": lax.rem(me + i, n)}, device_id_type=MESH)
        return carry

    lax.fori_loop(1, n, greet, 0, unroll=True)

    loads = [
        pltpu.make_async_copy(src, dst, load_sem.at[i])
        for i, (src, dst) in enumerate(
            [(small_hbm, small), (filt_hbm, filt), (proj_hbm, proj), (taps_hbm, taps), (skip_hbm, skip), (twiddle_hbm, twiddle), (first_hbm, first), (last_hbm, last)]
        )
    ]
    for load in loads:
        load.start()

    order_f = small.at[pl.ds(0, 256)]
    order_x = small.at[pl.ds(256, 256)]
    order_y = small.at[pl.ds(512, 256)]
    forward = small.at[pl.ds(768, 512)]
    inverse = small.at[pl.ds(1280, 256)]
    shifts = [small.at[pl.ds(1536, 256)], small.at[pl.ds(1792, 256)]]
    tails = [small.at[pl.ds(2048 + 16 * e, 16)] for e in range(3)]
    edges = [small.at[pl.ds(2096 + 16 * e, 16)] for e in range(3)]

    def at_peer(i):
        return lax.rem(me + i * 5, n)

    def arrange(i):
        owners = at_peer(2 * i), at_peer(2 * i + 1)
        sides = []
        for d in owners:
            rows = pl.ds(pl.multiple_of(d * own, own), own)
            sides.append([filt[part, rows, al * SIDE : (al + 1) * SIDE] for part in range(2) for al in range(a_lo)])
        stacked = jnp.concatenate([jnp.concatenate(side, axis=0) for side in sides], axis=1)
        arranged = dot(order_f[...], stacked).astype(bf16)
        for k, d in enumerate(owners):
            fsend[d] = arranged[:, k * SIDE : (k + 1) * SIDE]

    def f_rows(chunk):
        start, count = chunks[chunk]
        return pl.ds(start * 2 * cols, count * 2 * cols)

    def f_send(chunk, i):
        rows = f_rows(chunk)
        d = at_peer(i)
        pltpu.make_async_remote_copy(
            src_ref=fsend.at[d, rows], dst_ref=fbuf.at[me, rows], send_sem=fsend_sem.at[chunk], recv_sem=frecv_sem.at[chunk],
            device_id={"ctx": d}, device_id_type=MESH,
        ).start()

    def f_all(chunk):
        rows = f_rows(chunk)
        return pltpu.make_async_remote_copy(
            src_ref=fsend.at[pl.ds(0, n - 1), rows], dst_ref=fbuf.at[pl.ds(0, n - 1), rows],
            send_sem=fsend_sem.at[chunk], recv_sem=frecv_sem.at[chunk],
            device_id={"ctx": (me + 1) % n}, device_id_type=MESH,
        )

    loads[0].wait()
    loads[1].wait()

    def ahead(i, carry):
        arrange(i)
        return carry

    lax.fori_loop(0, AHEAD, ahead, 0)
    own_f = pltpu.make_async_copy(fsend.at[me], fbuf.at[me], own_sem.at[0])
    own_f.start()

    loads[2].wait()
    halo_out[...] = sum(dot_nt(tails[e][...], proj[e]) for e in range(3)).astype(bf16)

    pl.semaphore_wait(barrier, n - 1)

    halo = pltpu.make_async_remote_copy(
        src_ref=halo_out, dst_ref=halo_in, send_sem=hsend_sem, recv_sem=hrecv_sem,
        device_id={"ctx": (me + 1) % n}, device_id_type=MESH,
    )
    halo.start()

    def send_ready(i, carry):
        f_send(0, i)
        return carry

    lax.fori_loop(1, 2 * AHEAD, send_ready, 0)

    def arrange_send(i, carry):
        arrange(i)
        f_send(0, 2 * i)
        f_send(0, 2 * i + 1)
        return carry

    lax.fori_loop(AHEAD, n // 2, arrange_send, 0)

    loads[3].wait()
    loads[4].wait()
    halo.wait_recv()
    inside = jnp.where(me == 0, 0.0, 1.0).astype(f32)

    def gate(blk, carry):
        rows = pl.ds(pl.multiple_of(blk * SIDE, SIDE), SIDE)
        halo_rows = halo_in[:, rows]
        columns = jnp.concatenate(
            [taps[e, :, rows] for e in range(3)] + [skip[pl.ds(blk, 1), :], jnp.zeros((SIDE - 10, SIDE), f32)], axis=0
        ).T
        filtered = []
        for e in range(3):
            x = proj[e, rows, :]
            before = dot_tn(halo_rows, edges[e][...]) * inside
            back1, back2 = dot(x, shifts[0][...]), dot(x, shifts[1][...])
            back1 = jnp.concatenate([back1[:, :SIDE] + before[:, :SIDE], back1[:, SIDE:]], axis=1)
            back2 = jnp.concatenate([back2[:, :SIDE] + before[:, SIDE:], back2[:, SIDE:]], axis=1)
            tap = columns[:, 3 * e : 3 * e + 3]
            filtered.append(tap[:, 0:1] * x.astype(f32) + tap[:, 1:2] * back1 + tap[:, 2:3] * back2)
        product = (filtered[1] * filtered[2]).astype(bf16)
        owners = pl.ds(pl.multiple_of(blk * per_block, per_block), per_block)
        query[owners] = filtered[0].reshape(per_block, own, wide)
        direct[owners] = (columns[:, 9:10] * product.astype(f32)).reshape(per_block, own, wide)
        stacked = jnp.concatenate([product[:, s * SIDE : (s + 1) * SIDE] for s in range(s_lo)], axis=0)
        xsend[owners] = dot(order_x[...], stacked).astype(bf16).reshape(per_block, own * s_lo, SIDE)
        return carry

    lax.fori_loop(0, blocks, gate, 0)

    x_all = pltpu.make_async_remote_copy(
        src_ref=xsend.at[pl.ds(0, n - 1)], dst_ref=xbuf.at[pl.ds(0, n - 1)], send_sem=xsend_sem, recv_sem=xrecv_sem,
        device_id={"ctx": (me + 1) % n}, device_id_type=MESH,
    )

    def x_start(i, carry):
        d = at_peer(i)
        pltpu.make_async_remote_copy(
            src_ref=xsend.at[d], dst_ref=xbuf.at[me], send_sem=xsend_sem, recv_sem=xrecv_sem,
            device_id={"ctx": d}, device_id_type=MESH,
        ).start()
        return carry

    lax.fori_loop(1, n, x_start, 0)
    own_x = pltpu.make_async_copy(xsend.at[me], xbuf.at[me], own_sem.at[1])
    own_x.start()

    for chunk in range(1, len(chunks)):

        def f_start(i, carry, chunk=chunk):
            f_send(chunk, i)
            return carry

        lax.fori_loop(1, n, f_start, 0)

    for load in loads[5:]:
        load.wait()
    own_x.wait()
    x_all.wait_recv()
    cos, sin = twiddle[0:SIDE, :], twiddle[SIDE : 2 * SIDE, :]

    for g in range(groups):
        taken = xbuf[:, g * xrows : (g + 1) * xrows, :].astype(f32)
        for k in range(2):
            block = taken[:, k * some * s_lo : (k + 1) * some * s_lo, :].reshape(n * some * s_lo, SIDE)
            turned[(2 * g + k) * SIDE : (2 * g + k + 1) * SIDE, :] = block.T.astype(bf16)

    def over_s(g, carry):
        rows = pl.ds(pl.multiple_of(g * 2 * SIDE, 2 * SIDE), 2 * SIDE)
        for c in range(some):
            part = dot(turned[rows, :], first[:, c * 2 * SIDE : (c + 1) * 2 * SIDE])
            lanes = slice(c % 2 * SIDE, (c % 2 + 1) * SIDE)
            for k in range(2):
                re, im = part[k * SIDE : (k + 1) * SIDE, :SIDE], part[k * SIDE : (k + 1) * SIDE, SIDE:]
                pair = g * some + k * 2 + c // 2
                spec[pair, 0:SIDE, lanes] = (re * cos + im * sin).astype(bf16)
                spec[pair, SIDE : 2 * SIDE, lanes] = (im * cos - re * sin).astype(bf16)
        return carry

    lax.fori_loop(0, groups, over_s, 0)

    def over_r(i, carry):
        for k in range(2):
            values[2 * i + k] = dot(forward[...], spec[2 * i + k])
        return carry

    lax.fori_loop(0, own // 4, over_r, 0)

    own_f.wait()

    def through(h, k):
        for j in range(2):
            pair = 2 * h + j
            taken = fbuf[:, pl.ds(pl.multiple_of(pair * 2 * cols, 2 * cols), 2 * cols), :].astype(f32)
            shaped = []
            for c in range(2):
                gains = taken[:, c * cols : (c + 1) * cols, :]
                lanes = slice(c * SIDE, (c + 1) * SIDE)
                straight = values[pair, 0:half, lanes].reshape(n, cols, SIDE) * gains
                crossed = values[pair, half : 2 * half, lanes].reshape(n, cols, SIDE) * gains
                shaped.append((straight + pltpu.roll(crossed, a_lo, 1)).reshape(half, SIDE).astype(bf16))
            part = dot(inverse[...], jnp.concatenate(shaped, axis=1))
            rows = pl.ds(pl.multiple_of(k * SIDE, SIDE), SIDE)
            for c in range(2):
                re, im = part[:SIDE, c * SIDE : (c + 1) * SIDE], part[SIDE:, c * SIDE : (c + 1) * SIDE]
                at = (2 * j + c) * 2 * SIDE
                back[rows, at : at + SIDE] = (re * cos - im * sin).astype(bf16)
                back[rows, at + SIDE : at + 2 * SIDE] = (re * sin + im * cos).astype(bf16)

    def y_all(g):
        return pltpu.make_async_remote_copy(
            src_ref=ysend.at[g, pl.ds(0, (n - 1) * xrows)], dst_ref=ybuf.at[g, pl.ds(0, (n - 1) * xrows)],
            send_sem=ysend_sem.at[g], recv_sem=yrecv_sem.at[g], device_id={"ctx": (me + 1) % n}, device_id_type=MESH,
        )

    arrives = {start: chunk for chunk, (start, _) in enumerate(chunks)}
    own_y = []
    for g in range(groups):
        pairs = range(some * g, some * g + some)
        if pairs[0] in arrives:
            f_all(arrives[pairs[0]]).wait_recv()
        if pairs[2] in arrives:
            through(2 * g, 0)
            f_all(arrives[pairs[2]]).wait_recv()
            through(2 * g + 1, 1)
        else:

            def both(k, carry, g=g):
                through(2 * g + k, k)
                return carry

            lax.fori_loop(0, 2, both, 0)
        part = dot_nt(last[...], back[...])
        part = jnp.concatenate([part[:, k * SIDE : (k + 1) * SIDE].reshape(n, some * s_lo, SIDE) for k in range(2)], axis=1)
        ysend[g] = part.reshape(n * xrows, SIDE).astype(bf16)

        def y_start(i, carry, g=g):
            d = at_peer(i)
            pltpu.make_async_remote_copy(
                src_ref=ysend.at[g, pl.ds(pl.multiple_of(d * xrows, xrows), xrows)],
                dst_ref=ybuf.at[g, pl.ds(pl.multiple_of(me * xrows, xrows), xrows)],
                send_sem=ysend_sem.at[g], recv_sem=yrecv_sem.at[g], device_id={"ctx": d}, device_id_type=MESH,
            ).start()
            return carry

        lax.fori_loop(1, n, y_start, 0)
        mine = pl.ds(pl.multiple_of(me * xrows, xrows), xrows)
        own_y.append(pltpu.make_async_copy(ysend.at[g, mine], ybuf.at[g, mine], own_sem.at[2 + g]))
        own_y[g].start()

    owners = SIDE // GROUP
    for g in range(groups):
        own_y[g].wait()
        y_all(g).wait_recv()
        count = n // owners
        stacked = [ybuf[g, h * owners * xrows : (h + 1) * owners * xrows, :] for h in range(count)]
        arranged = dot(order_y[...], jnp.concatenate(stacked, axis=1))
        for h in range(count):
            for s in range(s_lo):
                conv[h * owners : (h + 1) * owners, g * GROUP : (g + 1) * GROUP, s * SIDE : (s + 1) * SIDE] = arranged[
                    s * SIDE : (s + 1) * SIDE, h * SIDE : (h + 1) * SIDE
                ].reshape(owners, GROUP, SIDE)
        if g % 2 == 1:
            rows = slice((g - 1) * GROUP, (g + 1) * GROUP)
            out[:, rows, :] = (query[:, rows, :] * (conv[:, rows, :] + direct[:, rows, :])).astype(bf16)

    halo.wait_send()
    x_all.wait_send()
    for chunk in range(len(chunks)):
        f_all(chunk).wait_send()
    for g in range(groups):
        y_all(g).wait_send()


def shards(projections, short_filter, skip_gain, filter_spectra):
    n = lax.axis_size("ctx")
    channels, tokens = projections.shape[1:]
    freqs = filter_spectra.shape[2]
    own, s_lo, a_lo = channels // n, tokens // SIDE, freqs // SIDE
    groups = own // GROUP
    cols = 2 * a_lo
    pairs = own // 2
    chunks = [(0, pairs // 2), (pairs // 2, pairs // 4), (pairs * 3 // 4, pairs // 8), (pairs * 7 // 8, pairs // 8)]
    hbm, vmem = pl.BlockSpec(memory_space=pltpu.HBM), pl.BlockSpec(memory_space=pltpu.VMEM)
    small, twiddle, first, last = tables(n, own, s_lo, a_lo)
    dma = pltpu.SemaphoreType.DMA
    operands = [
        filter_spectra, projections, jnp.swapaxes(short_filter, 1, 2), skip_gain.reshape(channels // SIDE, SIDE),
        *(jnp.asarray(table) for table in (small, twiddle, first, last)),
    ]
    return pl.pallas_call(
        functools.partial(kernel, n, own, s_lo, a_lo, chunks),
        out_shape=jax.ShapeDtypeStruct((n, own, tokens), bf16),
        in_specs=[hbm] * 8,
        out_specs=vmem,
        scratch_shapes=[
            pltpu.VMEM(filter_spectra.shape, bf16),
            pltpu.VMEM(projections.shape, bf16),
            pltpu.VMEM((3, 3, channels), f32),
            pltpu.VMEM((channels // SIDE, SIDE), f32),
            pltpu.VMEM(small.shape, bf16),
            pltpu.VMEM(twiddle.shape, f32),
            pltpu.VMEM(first.shape, bf16),
            pltpu.VMEM(last.shape, bf16),
            pltpu.VMEM((n, own * cols, SIDE), bf16),
            pltpu.VMEM((n, own * cols, SIDE), bf16),
            pltpu.VMEM((n, own * s_lo, SIDE), bf16),
            pltpu.VMEM((n, own * s_lo, SIDE), bf16),
            pltpu.VMEM((groups, n * GROUP * s_lo, SIDE), bf16),
            pltpu.VMEM((groups, n * GROUP * s_lo, SIDE), bf16),
            pltpu.VMEM((2 * groups * SIDE, n * GROUP * s_lo // 2), bf16),
            pltpu.VMEM((own // 2, 2 * SIDE, 2 * SIDE), bf16),
            pltpu.VMEM((own // 2, 4 * SIDE, 2 * SIDE), f32),
            pltpu.VMEM((2 * SIDE, GROUP * SIDE), bf16),
            pltpu.VMEM((n, own, tokens), f32),
            pltpu.VMEM((n, own, tokens), f32),
            pltpu.VMEM((n, own, tokens), f32),
            pltpu.VMEM((16, channels), bf16),
            pltpu.VMEM((16, channels), bf16),
            dma((8,)),
            dma((2 + groups,)),
            dma((len(chunks),)),
            dma((len(chunks),)),
            dma,
            dma,
            dma((groups,)),
            dma((groups,)),
            dma,
            dma,
        ],
        compiler_params=pltpu.CompilerParams(collective_id=0, has_side_effects=True, vmem_limit_bytes=52 << 20),
        cost_estimate=pl.CostEstimate(flops=6_000_000_000, bytes_accessed=12_000_000, transcendentals=0),
    )(*(pltpu.with_memory_space_constraint(x, pltpu.HBM) for x in operands)).reshape(channels, tokens)


def solution(mesh):
    return jax.shard_map(
        shards,
        mesh=mesh,
        in_specs=(P(None, "ch", "ctx"), P(None, "ch", None), P("ch"), P(None, "ch", "ctx")),
        out_specs=P("ch", "ctx"),
        check_vma=False,
    )
```

```python
import functools

import jax
import jax.numpy as jnp
import ml_dtypes
import numpy as np
from jax import lax
from jax.experimental import pallas as pl
from jax.experimental.pallas import tpu as pltpu
from jax.sharding import PartitionSpec as P

MESH = pl.DeviceIdType.MESH
SIDE = 128
GROUP = 8
AHEAD = 3
f32, bf16 = jnp.float32, jnp.bfloat16


def tables(n, own, s_lo, a_lo):
    period = SIDE * SIDE
    cols = 2 * a_lo
    wide = SIDE * s_lo
    order_f = np.zeros((own * cols, own * cols))
    c, j = np.meshgrid(np.arange(own), np.arange(cols), indexing="ij")
    order_f[(c * cols + j).ravel(), (j * own + c).ravel()] = 1
    order_x = np.zeros((wide, wide))
    c, s = np.meshgrid(np.arange(SIDE), np.arange(s_lo), indexing="ij")
    order_x[(c * s_lo + s).ravel(), (s * SIDE + c).ravel()] = 1
    order_y = np.zeros((wide, wide))
    q, c, s = np.meshgrid(np.arange(SIDE // GROUP), np.arange(GROUP), np.arange(s_lo), indexing="ij")
    order_y[(s * SIDE + q * GROUP + c).ravel(), ((q * GROUP + c) * s_lo + s).ravel()] = 1
    q, part, al = (v.ravel() for v in np.meshgrid(np.arange(n), np.arange(2), np.arange(a_lo), indexing="ij"))
    angle = 2 * np.pi * ((q * a_lo + al)[:, None] * np.arange(SIDE)[None, :] % SIDE) / SIDE
    wr, wi = np.cos(angle), -np.sin(angle)
    sign = np.where(part == 1, -1.0, 1.0)[:, None]
    forward = np.concatenate([np.concatenate([wr, -wi], 1), np.concatenate([wi, wr], 1) * sign], 0)
    vr, vi = np.cos(angle).T, np.sin(angle).T
    real = (part == 0)[None, :]
    inverse = np.concatenate([np.where(real, vr, -vi), np.where(real, vi, vr)], 0)
    tail = np.zeros((3, 16, wide))
    edge = np.zeros((3, 16, 2 * SIDE))
    for e in range(3):
        tail[e, 2 * e, wide - 2] = 1
        tail[e, 2 * e + 1, wide - 1] = 1
        edge[e, 2 * e + 1, 0] = 1
        edge[e, 2 * e, SIDE] = 1
        edge[e, 2 * e + 1, SIDE + 1] = 1
    shifts = [np.eye(wide, k=by) for by in (1, 2)]
    small = np.concatenate(
        [order_f, order_x, order_y, forward, inverse, *shifts, tail.reshape(48, -1), edge.reshape(48, -1)], 0
    )
    some = GROUP // 2
    s = np.arange(n * s_lo)
    angle = 2 * np.pi * (s[:, None] * np.arange(SIDE)[None, :] % SIDE) / SIDE
    first = np.zeros((n, some, s_lo, some, 2, SIDE))
    for g in range(some):
        first[:, g, :, g, 0] = np.cos(angle).reshape(n, s_lo, SIDE)
        first[:, g, :, g, 1] = -np.sin(angle).reshape(n, s_lo, SIDE)
    first = first.reshape(n * some * s_lo, some * 2 * SIDE)
    last = first / period
    angle = 2 * np.pi * np.arange(SIDE)[:, None] * np.arange(SIDE)[None, :] / period
    twiddle = np.concatenate([np.cos(angle), np.sin(angle)], 0)
    return [
        small.astype(ml_dtypes.bfloat16),
        twiddle.astype(np.float32),
        first.astype(ml_dtypes.bfloat16),
        last.astype(ml_dtypes.bfloat16),
    ]


def dot(a, b):
    return jnp.dot(a, b, preferred_element_type=f32)


def dot_nt(a, b):
    return lax.dot_general(a, b, (((1,), (1,)), ((), ())), preferred_element_type=f32)


def dot_tn(a, b):
    return lax.dot_general(a, b, (((0,), (0,)), ((), ())), preferred_element_type=f32)


def kernel(
    n, own, s_lo, a_lo, chunks, returns,
    filt_hbm, proj_hbm, taps_hbm, skip_hbm, small_hbm, twiddle_hbm, first_hbm, last_hbm,
    out,
    filt, proj, taps, skip, small, twiddle, first, last,
    fsend, fbuf, xsend, xbuf, ysend, ybuf, turned, spec, values, back, conv, query, direct, halo_out, halo_in,
    load_sem, own_sem, fsend_sem, frecv_sem, xsend_sem, xrecv_sem, ysend_sem, yrecv_sem, hsend_sem, hrecv_sem,
):
    me = lax.axis_index("ctx")
    groups = own // GROUP
    cols = 2 * a_lo
    some = GROUP // 2
    xrows = GROUP * s_lo
    blocks = n * own // SIDE
    per_block = SIDE // own
    half = n * cols
    wide = SIDE * s_lo

    barrier = pltpu.get_barrier_semaphore()

    def greet(i, carry):
        pl.semaphore_signal(barrier, inc=1, device_id={"ctx": lax.rem(me + i, n)}, device_id_type=MESH)
        return carry

    lax.fori_loop(1, n, greet, 0, unroll=True)

    head, rest = pl.ds(0, 256), pl.ds(256, small.shape[0] - 256)
    load_head, load_filt, load_proj, load_rest, load_taps, load_skip, *load_late = [
        pltpu.make_async_copy(src, dst, load_sem.at[i])
        for i, (src, dst) in enumerate(
            [
                (small_hbm.at[head], small.at[head]), (filt_hbm, filt), (proj_hbm, proj), (small_hbm.at[rest], small.at[rest]),
                (taps_hbm, taps), (skip_hbm, skip), (twiddle_hbm, twiddle), (first_hbm, first), (last_hbm, last),
            ]
        )
    ]
    load_head.start()
    load_filt.start()

    order_f = small.at[pl.ds(0, 256)]
    order_x = small.at[pl.ds(256, 256)]
    order_y = small.at[pl.ds(512, 256)]
    forward = small.at[pl.ds(768, 512)]
    inverse = small.at[pl.ds(1280, 256)]
    shifts = [small.at[pl.ds(1536, 256)], small.at[pl.ds(1792, 256)]]
    tails = [small.at[pl.ds(2048 + 16 * e, 16)] for e in range(3)]
    edges = [small.at[pl.ds(2096 + 16 * e, 16)] for e in range(3)]

    def at_peer(i):
        return lax.rem(me + i * 5, n)

    def arrange(i):
        owners = at_peer(2 * i), at_peer(2 * i + 1)
        sides = []
        for d in owners:
            rows = pl.ds(pl.multiple_of(d * own, own), own)
            sides.append([filt[part, rows, al * SIDE : (al + 1) * SIDE] for part in range(2) for al in range(a_lo)])
        stacked = jnp.concatenate([jnp.concatenate(side, axis=0) for side in sides], axis=1)
        arranged = dot(order_f[...], stacked).astype(bf16)
        for k, d in enumerate(owners):
            fsend[d] = arranged[:, k * SIDE : (k + 1) * SIDE]

    def f_rows(chunk):
        start, count = chunks[chunk]
        return pl.ds(start * 2 * cols, count * 2 * cols)

    def f_send(chunk, i):
        rows = f_rows(chunk)
        d = at_peer(i)
        pltpu.make_async_remote_copy(
            src_ref=fsend.at[d, rows], dst_ref=fbuf.at[me, rows], send_sem=fsend_sem.at[chunk], recv_sem=frecv_sem.at[chunk],
            device_id={"ctx": d}, device_id_type=MESH,
        ).start()

    def f_all(chunk):
        rows = f_rows(chunk)
        return pltpu.make_async_remote_copy(
            src_ref=fsend.at[pl.ds(0, n - 1), rows], dst_ref=fbuf.at[pl.ds(0, n - 1), rows],
            send_sem=fsend_sem.at[chunk], recv_sem=frecv_sem.at[chunk],
            device_id={"ctx": (me + 1) % n}, device_id_type=MESH,
        )

    load_head.wait()
    load_filt.wait()
    for load in (load_proj, load_rest, load_taps, load_skip, *load_late):
        load.start()

    def ahead(i, carry):
        arrange(i)
        return carry

    lax.fori_loop(0, AHEAD, ahead, 0)
    own_f = pltpu.make_async_copy(fsend.at[me], fbuf.at[me], own_sem.at[0])
    own_f.start()

    pl.semaphore_wait(barrier, n - 1)

    def send_ready(i, carry):
        f_send(0, i)
        return carry

    lax.fori_loop(1, 2 * AHEAD, send_ready, 0)

    load_proj.wait()
    load_rest.wait()
    halo_out[...] = sum(dot_nt(tails[e][...], proj[e]) for e in range(3)).astype(bf16)
    halo = pltpu.make_async_remote_copy(
        src_ref=halo_out, dst_ref=halo_in, send_sem=hsend_sem, recv_sem=hrecv_sem,
        device_id={"ctx": (me + 1) % n}, device_id_type=MESH,
    )
    halo.start()

    def arrange_send(i, carry):
        arrange(i)
        f_send(0, 2 * i)
        f_send(0, 2 * i + 1)
        return carry

    lax.fori_loop(AHEAD, n // 2, arrange_send, 0)

    load_taps.wait()
    load_skip.wait()
    halo.wait_recv()
    inside = jnp.where(me == 0, 0.0, 1.0).astype(f32)

    def gate(blk, carry):
        rows = pl.ds(pl.multiple_of(blk * SIDE, SIDE), SIDE)
        halo_rows = halo_in[:, rows]
        columns = jnp.concatenate(
            [taps[e, :, rows] for e in range(3)] + [skip[pl.ds(blk, 1), :], jnp.zeros((SIDE - 10, SIDE), f32)], axis=0
        ).T
        filtered = []
        for e in range(3):
            x = proj[e, rows, :]
            before = dot_tn(halo_rows, edges[e][...]) * inside
            back1, back2 = dot(x, shifts[0][...]), dot(x, shifts[1][...])
            back1 = jnp.concatenate([back1[:, :SIDE] + before[:, :SIDE], back1[:, SIDE:]], axis=1)
            back2 = jnp.concatenate([back2[:, :SIDE] + before[:, SIDE:], back2[:, SIDE:]], axis=1)
            tap = columns[:, 3 * e : 3 * e + 3]
            filtered.append(tap[:, 0:1] * x.astype(f32) + tap[:, 1:2] * back1 + tap[:, 2:3] * back2)
        product = (filtered[1] * filtered[2]).astype(bf16)
        owners = pl.ds(pl.multiple_of(blk * per_block, per_block), per_block)
        query[owners] = filtered[0].reshape(per_block, own, wide)
        direct[owners] = (columns[:, 9:10] * product.astype(f32)).reshape(per_block, own, wide)
        stacked = jnp.concatenate([product[:, s * SIDE : (s + 1) * SIDE] for s in range(s_lo)], axis=0)
        xsend[owners] = dot(order_x[...], stacked).astype(bf16).reshape(per_block, own * s_lo, SIDE)
        return carry

    lax.fori_loop(0, blocks, gate, 0)

    x_all = pltpu.make_async_remote_copy(
        src_ref=xsend.at[pl.ds(0, n - 1)], dst_ref=xbuf.at[pl.ds(0, n - 1)], send_sem=xsend_sem, recv_sem=xrecv_sem,
        device_id={"ctx": (me + 1) % n}, device_id_type=MESH,
    )

    def x_start(i, carry):
        d = at_peer(i)
        pltpu.make_async_remote_copy(
            src_ref=xsend.at[d], dst_ref=xbuf.at[me], send_sem=xsend_sem, recv_sem=xrecv_sem,
            device_id={"ctx": d}, device_id_type=MESH,
        ).start()
        return carry

    lax.fori_loop(1, n, x_start, 0)
    own_x = pltpu.make_async_copy(xsend.at[me], xbuf.at[me], own_sem.at[1])
    own_x.start()

    for chunk in range(1, len(chunks)):

        def f_start(i, carry, chunk=chunk):
            f_send(chunk, i)
            return carry

        lax.fori_loop(1, n, f_start, 0)

    for load in load_late:
        load.wait()
    own_x.wait()
    x_all.wait_recv()
    cos, sin = twiddle[0:SIDE, :], twiddle[SIDE : 2 * SIDE, :]

    for g in range(groups):
        taken = xbuf[:, g * xrows : (g + 1) * xrows, :].astype(f32)
        for k in range(2):
            block = taken[:, k * some * s_lo : (k + 1) * some * s_lo, :].reshape(n * some * s_lo, SIDE)
            turned[(2 * g + k) * SIDE : (2 * g + k + 1) * SIDE, :] = block.T.astype(bf16)

    def over_s(g, carry):
        rows = pl.ds(pl.multiple_of(g * 2 * SIDE, 2 * SIDE), 2 * SIDE)
        for c in range(some):
            part = dot(turned[rows, :], first[:, c * 2 * SIDE : (c + 1) * 2 * SIDE])
            lanes = slice(c % 2 * SIDE, (c % 2 + 1) * SIDE)
            for k in range(2):
                re, im = part[k * SIDE : (k + 1) * SIDE, :SIDE], part[k * SIDE : (k + 1) * SIDE, SIDE:]
                pair = g * some + k * 2 + c // 2
                spec[pair, 0:SIDE, lanes] = (re * cos + im * sin).astype(bf16)
                spec[pair, SIDE : 2 * SIDE, lanes] = (im * cos - re * sin).astype(bf16)
        return carry

    lax.fori_loop(0, groups, over_s, 0)

    def over_r(i, carry):
        for k in range(2):
            values[2 * i + k] = dot(forward[...], spec[2 * i + k])
        return carry

    lax.fori_loop(0, own // 4, over_r, 0)

    own_f.wait()

    def through(h, k):
        for j in range(2):
            pair = 2 * h + j
            taken = fbuf[:, pl.ds(pl.multiple_of(pair * 2 * cols, 2 * cols), 2 * cols), :].astype(f32)
            shaped = []
            for c in range(2):
                gains = taken[:, c * cols : (c + 1) * cols, :]
                lanes = slice(c * SIDE, (c + 1) * SIDE)
                straight = values[pair, 0:half, lanes].reshape(n, cols, SIDE) * gains
                crossed = values[pair, half : 2 * half, lanes].reshape(n, cols, SIDE) * gains
                shaped.append((straight + pltpu.roll(crossed, a_lo, 1)).reshape(half, SIDE).astype(bf16))
            part = dot(inverse[...], jnp.concatenate(shaped, axis=1))
            rows = pl.ds(pl.multiple_of(k * SIDE, SIDE), SIDE)
            for c in range(2):
                re, im = part[:SIDE, c * SIDE : (c + 1) * SIDE], part[SIDE:, c * SIDE : (c + 1) * SIDE]
                at = (2 * j + c) * 2 * SIDE
                back[rows, at : at + SIDE] = (re * cos - im * sin).astype(bf16)
                back[rows, at + SIDE : at + 2 * SIDE] = (re * sin + im * cos).astype(bf16)

    def y_copy(k, src, dst, d):
        rows = pl.ds(returns[k][0] * xrows, returns[k][1] * xrows)
        return pltpu.make_async_remote_copy(
            src_ref=ysend.at[src, rows], dst_ref=ybuf.at[dst, rows], send_sem=ysend_sem.at[k], recv_sem=yrecv_sem.at[k],
            device_id={"ctx": d}, device_id_type=MESH,
        )

    def y_all(k):
        return y_copy(k, pl.ds(0, n - 1), pl.ds(0, n - 1), (me + 1) % n)

    sends = {start + count - 1: k for k, (start, count) in enumerate(returns)}
    arrives = {start: chunk for chunk, (start, _) in enumerate(chunks)}
    own_y = []
    for g in range(groups):
        pairs = range(some * g, some * g + some)
        if pairs[0] in arrives:
            f_all(arrives[pairs[0]]).wait_recv()
        if pairs[2] in arrives:
            through(2 * g, 0)
            early = dot_nt(last[...], back[0:SIDE, :])
            f_all(arrives[pairs[2]]).wait_recv()
            through(2 * g + 1, 1)
            parts = [early, dot_nt(last[...], back[SIDE : 2 * SIDE, :])]
        else:

            def both(k, carry, g=g):
                through(2 * g + k, k)
                return carry

            lax.fori_loop(0, 2, both, 0)
            part = dot_nt(last[...], back[...])
            parts = [part[:, k * SIDE : (k + 1) * SIDE] for k in range(2)]
        part = jnp.concatenate([part.reshape(n, some * s_lo, SIDE) for part in parts], axis=1)
        ysend[:, g * xrows : (g + 1) * xrows, :] = part.astype(bf16)
        if g not in sends:
            continue

        def y_start(i, carry, k=sends[g]):
            d = at_peer(i)
            y_copy(k, d, me, d).start()
            return carry

        lax.fori_loop(1, n, y_start, 0)
        start, count = returns[sends[g]]
        mine = pl.ds(start * xrows, count * xrows)
        own_y.append(pltpu.make_async_copy(ysend.at[me, mine], ybuf.at[me, mine], own_sem.at[2 + sends[g]]))
        own_y[-1].start()

    owners = SIDE // GROUP
    for g in range(groups):
        for k, (start, _) in enumerate(returns):
            if g == start:
                own_y[k].wait()
                y_all(k).wait_recv()
        count = n // owners
        stacked = [
            ybuf[h * owners : (h + 1) * owners, g * xrows : (g + 1) * xrows, :].reshape(owners * xrows, SIDE) for h in range(count)
        ]
        arranged = dot(order_y[...], jnp.concatenate(stacked, axis=1))
        for h in range(count):
            for s in range(s_lo):
                conv[h * owners : (h + 1) * owners, g * GROUP : (g + 1) * GROUP, s * SIDE : (s + 1) * SIDE] = arranged[
                    s * SIDE : (s + 1) * SIDE, h * SIDE : (h + 1) * SIDE
                ].reshape(owners, GROUP, SIDE)
        if g % 2 == 1:
            rows = slice((g - 1) * GROUP, (g + 1) * GROUP)
            out[:, rows, :] = (query[:, rows, :] * (conv[:, rows, :] + direct[:, rows, :])).astype(bf16)

    halo.wait_send()
    x_all.wait_send()
    for chunk in range(len(chunks)):
        f_all(chunk).wait_send()
    for k in range(len(returns)):
        y_all(k).wait_send()


def shards(projections, short_filter, skip_gain, filter_spectra):
    n = lax.axis_size("ctx")
    channels, tokens = projections.shape[1:]
    freqs = filter_spectra.shape[2]
    own, s_lo, a_lo = channels // n, tokens // SIDE, freqs // SIDE
    groups = own // GROUP
    cols = 2 * a_lo
    pairs = own // 2
    chunks = [(0, pairs // 2), (pairs // 2, pairs // 4), (pairs * 3 // 4, pairs // 8), (pairs * 7 // 8, pairs // 8)]
    returns = [(0, groups * 3 // 4), (groups * 3 // 4, groups // 4)]
    hbm, vmem = pl.BlockSpec(memory_space=pltpu.HBM), pl.BlockSpec(memory_space=pltpu.VMEM)
    small, twiddle, first, last = tables(n, own, s_lo, a_lo)
    dma = pltpu.SemaphoreType.DMA
    operands = [
        filter_spectra, projections, jnp.swapaxes(short_filter, 1, 2), skip_gain.reshape(channels // SIDE, SIDE),
        *(jnp.asarray(table) for table in (small, twiddle, first, last)),
    ]
    return pl.pallas_call(
        functools.partial(kernel, n, own, s_lo, a_lo, chunks, returns),
        out_shape=jax.ShapeDtypeStruct((n, own, tokens), bf16),
        in_specs=[hbm] * 8,
        out_specs=vmem,
        scratch_shapes=[
            pltpu.VMEM(filter_spectra.shape, bf16),
            pltpu.VMEM(projections.shape, bf16),
            pltpu.VMEM((3, 3, channels), f32),
            pltpu.VMEM((channels // SIDE, SIDE), f32),
            pltpu.VMEM(small.shape, bf16),
            pltpu.VMEM(twiddle.shape, f32),
            pltpu.VMEM(first.shape, bf16),
            pltpu.VMEM(last.shape, bf16),
            pltpu.VMEM((n, own * cols, SIDE), bf16),
            pltpu.VMEM((n, own * cols, SIDE), bf16),
            pltpu.VMEM((n, own * s_lo, SIDE), bf16),
            pltpu.VMEM((n, own * s_lo, SIDE), bf16),
            pltpu.VMEM((n, own * s_lo, SIDE), bf16),
            pltpu.VMEM((n, own * s_lo, SIDE), bf16),
            pltpu.VMEM((2 * groups * SIDE, n * GROUP * s_lo // 2), bf16),
            pltpu.VMEM((own // 2, 2 * SIDE, 2 * SIDE), bf16),
            pltpu.VMEM((own // 2, 4 * SIDE, 2 * SIDE), f32),
            pltpu.VMEM((2 * SIDE, GROUP * SIDE), bf16),
            pltpu.VMEM((n, own, tokens), f32),
            pltpu.VMEM((n, own, tokens), f32),
            pltpu.VMEM((n, own, tokens), f32),
            pltpu.VMEM((16, channels), bf16),
            pltpu.VMEM((16, channels), bf16),
            dma((9,)),
            dma((2 + len(returns),)),
            dma((len(chunks),)),
            dma((len(chunks),)),
            dma,
            dma,
            dma((len(returns),)),
            dma((len(returns),)),
            dma,
            dma,
        ],
        compiler_params=pltpu.CompilerParams(collective_id=0, has_side_effects=True, vmem_limit_bytes=52 << 20),
        cost_estimate=pl.CostEstimate(flops=6_000_000_000, bytes_accessed=12_000_000, transcendentals=0),
    )(*(pltpu.with_memory_space_constraint(x, pltpu.HBM) for x in operands)).reshape(channels, tokens)


def solution(mesh):
    return jax.shard_map(
        shards,
        mesh=mesh,
        in_specs=(P(None, "ch", "ctx"), P(None, "ch", None), P("ch"), P(None, "ch", "ctx")),
        out_specs=P("ch", "ctx"),
        check_vma=False,
    )
```

```python
import functools

import jax
import jax.numpy as jnp
import ml_dtypes
import numpy as np
from jax import lax
from jax.experimental import pallas as pl
from jax.experimental.pallas import tpu as pltpu
from jax.sharding import PartitionSpec as P

MESH = pl.DeviceIdType.MESH
SIDE = 128
GROUP = 8
AHEAD = 3
f32, bf16 = jnp.float32, jnp.bfloat16


def tables(n, own, s_lo, a_lo):
    period = SIDE * SIDE
    cols = 2 * a_lo
    wide = SIDE * s_lo
    order_f = np.zeros((own * cols, own * cols))
    c, j = np.meshgrid(np.arange(own), np.arange(cols), indexing="ij")
    order_f[(c * cols + j).ravel(), (j * own + c).ravel()] = 1
    order_x = np.zeros((wide, wide))
    c, s = np.meshgrid(np.arange(SIDE), np.arange(s_lo), indexing="ij")
    order_x[(c * s_lo + s).ravel(), (s * SIDE + c).ravel()] = 1
    order_y = np.zeros((wide, wide))
    q, c, s = np.meshgrid(np.arange(SIDE // GROUP), np.arange(GROUP), np.arange(s_lo), indexing="ij")
    order_y[(s * SIDE + q * GROUP + c).ravel(), ((q * GROUP + c) * s_lo + s).ravel()] = 1
    q, part, al = (v.ravel() for v in np.meshgrid(np.arange(n), np.arange(2), np.arange(a_lo), indexing="ij"))
    angle = 2 * np.pi * ((q * a_lo + al)[:, None] * np.arange(SIDE)[None, :] % SIDE) / SIDE
    wr, wi = np.cos(angle), -np.sin(angle)
    sign = np.where(part == 1, -1.0, 1.0)[:, None]
    forward = np.concatenate([np.concatenate([wr, -wi], 1), np.concatenate([wi, wr], 1) * sign], 0)
    vr, vi = np.cos(angle).T, np.sin(angle).T
    real = (part == 0)[None, :]
    inverse = np.concatenate([np.where(real, vr, -vi), np.where(real, vi, vr)], 0)
    tail = np.zeros((3, 16, wide))
    edge = np.zeros((3, 16, 2 * SIDE))
    for e in range(3):
        tail[e, 2 * e, wide - 2] = 1
        tail[e, 2 * e + 1, wide - 1] = 1
        edge[e, 2 * e + 1, 0] = 1
        edge[e, 2 * e, SIDE] = 1
        edge[e, 2 * e + 1, SIDE + 1] = 1
    shifts = [np.eye(wide, k=by) for by in (1, 2)]
    small = np.concatenate(
        [order_f, order_x, order_y, forward, inverse, *shifts, tail.reshape(48, -1), edge.reshape(48, -1)], 0
    )
    some = GROUP // 2
    s = np.arange(n * s_lo)
    angle = 2 * np.pi * (s[:, None] * np.arange(SIDE)[None, :] % SIDE) / SIDE
    first = np.zeros((n, some, s_lo, some, 2, SIDE))
    for g in range(some):
        first[:, g, :, g, 0] = np.cos(angle).reshape(n, s_lo, SIDE)
        first[:, g, :, g, 1] = -np.sin(angle).reshape(n, s_lo, SIDE)
    first = first.reshape(n * some * s_lo, some * 2 * SIDE)
    last = first / period
    angle = 2 * np.pi * np.arange(SIDE)[:, None] * np.arange(SIDE)[None, :] / period
    twiddle = np.concatenate([np.cos(angle), np.sin(angle)], 0)
    return [
        small.astype(ml_dtypes.bfloat16),
        twiddle.astype(np.float32),
        first.astype(ml_dtypes.bfloat16),
        last.astype(ml_dtypes.bfloat16),
    ]


def dot(a, b):
    return jnp.dot(a, b, preferred_element_type=f32)


def dot_nt(a, b):
    return lax.dot_general(a, b, (((1,), (1,)), ((), ())), preferred_element_type=f32)


def dot_tn(a, b):
    return lax.dot_general(a, b, (((0,), (0,)), ((), ())), preferred_element_type=f32)


def kernel(
    n, own, s_lo, a_lo, chunks, returns,
    filt_hbm, proj_hbm, taps_hbm, skip_hbm, small_hbm, twiddle_hbm, first_hbm, last_hbm,
    out,
    filt, proj, taps, skip, small, twiddle, first, last,
    fsend, fbuf, xsend, xbuf, ysend, ybuf, turned, spec, values, back, conv, query, direct, halo_out, halo_in,
    load_sem, own_sem, fsend_sem, frecv_sem, xsend_sem, xrecv_sem, ysend_sem, yrecv_sem, hsend_sem, hrecv_sem,
):
    me = lax.axis_index("ctx")
    groups = own // GROUP
    cols = 2 * a_lo
    some = GROUP // 2
    xrows = GROUP * s_lo
    blocks = n * own // SIDE
    per_block = SIDE // own
    half = n * cols
    wide = SIDE * s_lo

    barrier = pltpu.get_barrier_semaphore()

    def greet(i, carry):
        pl.semaphore_signal(barrier, inc=1, device_id={"ctx": lax.rem(me + i, n)}, device_id_type=MESH)
        return carry

    lax.fori_loop(1, n, greet, 0, unroll=True)

    head, rest = pl.ds(0, 256), pl.ds(256, small.shape[0] - 256)
    load_head, load_filt, load_proj, load_rest, load_taps, load_skip, *load_late = [
        pltpu.make_async_copy(src, dst, load_sem.at[i])
        for i, (src, dst) in enumerate(
            [
                (small_hbm.at[head], small.at[head]), (filt_hbm, filt), (proj_hbm, proj), (small_hbm.at[rest], small.at[rest]),
                (taps_hbm, taps), (skip_hbm, skip), (twiddle_hbm, twiddle), (first_hbm, first), (last_hbm, last),
            ]
        )
    ]
    load_head.start()
    load_filt.start()

    order_f = small.at[pl.ds(0, 256)]
    order_x = small.at[pl.ds(256, 256)]
    order_y = small.at[pl.ds(512, 256)]
    forward = small.at[pl.ds(768, 512)]
    inverse = small.at[pl.ds(1280, 256)]
    shifts = [small.at[pl.ds(1536, 256)], small.at[pl.ds(1792, 256)]]
    tails = [small.at[pl.ds(2048 + 16 * e, 16)] for e in range(3)]
    edges = [small.at[pl.ds(2096 + 16 * e, 16)] for e in range(3)]

    def at_peer(i):
        return lax.rem(me + i * 5, n)

    def arrange(i):
        owners = at_peer(2 * i), at_peer(2 * i + 1)
        sides = []
        for d in owners:
            rows = pl.ds(pl.multiple_of(d * own, own), own)
            sides.append([filt[part, rows, al * SIDE : (al + 1) * SIDE] for part in range(2) for al in range(a_lo)])
        stacked = jnp.concatenate([jnp.concatenate(side, axis=0) for side in sides], axis=1)
        arranged = dot(order_f[...], stacked).astype(bf16)
        for k, d in enumerate(owners):
            fsend[d] = arranged[:, k * SIDE : (k + 1) * SIDE]

    def f_rows(chunk):
        start, count = chunks[chunk]
        return pl.ds(start * 2 * cols, count * 2 * cols)

    def f_send(chunk, i):
        rows = f_rows(chunk)
        d = at_peer(i)
        pltpu.make_async_remote_copy(
            src_ref=fsend.at[d, rows], dst_ref=fbuf.at[me, rows], send_sem=fsend_sem.at[chunk], recv_sem=frecv_sem.at[chunk],
            device_id={"ctx": d}, device_id_type=MESH,
        ).start()

    def f_all(chunk):
        rows = f_rows(chunk)
        return pltpu.make_async_remote_copy(
            src_ref=fsend.at[pl.ds(0, n - 1), rows], dst_ref=fbuf.at[pl.ds(0, n - 1), rows],
            send_sem=fsend_sem.at[chunk], recv_sem=frecv_sem.at[chunk],
            device_id={"ctx": (me + 1) % n}, device_id_type=MESH,
        )

    load_head.wait()
    load_filt.wait()
    for load in (load_proj, load_rest, load_taps, load_skip, *load_late):
        load.start()

    def ahead(i, carry):
        arrange(i)
        return carry

    lax.fori_loop(0, AHEAD, ahead, 0)
    own_f = pltpu.make_async_copy(fsend.at[me], fbuf.at[me], own_sem.at[0])
    own_f.start()

    pl.semaphore_wait(barrier, n - 1)

    def send_ready(i, carry):
        f_send(0, i)
        return carry

    lax.fori_loop(1, 2 * AHEAD, send_ready, 0)

    load_proj.wait()
    load_rest.wait()
    halo_out[...] = sum(dot_nt(tails[e][...], proj[e]) for e in range(3)).astype(bf16)
    halo = pltpu.make_async_remote_copy(
        src_ref=halo_out, dst_ref=halo_in, send_sem=hsend_sem, recv_sem=hrecv_sem,
        device_id={"ctx": (me + 1) % n}, device_id_type=MESH,
    )
    halo.start()

    def arrange_send(i, carry):
        arrange(i)
        f_send(0, 2 * i)
        f_send(0, 2 * i + 1)
        return carry

    lax.fori_loop(AHEAD, n // 2, arrange_send, 0)

    load_taps.wait()
    load_skip.wait()
    halo.wait_recv()
    inside = jnp.where(me == 0, 0.0, 1.0).astype(f32)

    def gate(blk, carry):
        rows = pl.ds(pl.multiple_of(blk * SIDE, SIDE), SIDE)
        halo_rows = halo_in[:, rows]
        columns = jnp.concatenate(
            [taps[e, :, rows] for e in range(3)] + [skip[pl.ds(blk, 1), :], jnp.zeros((SIDE - 10, SIDE), f32)], axis=0
        ).T
        filtered = []
        for e in range(3):
            x = proj[e, rows, :]
            before = dot_tn(halo_rows, edges[e][...]) * inside
            back1, back2 = dot(x, shifts[0][...]), dot(x, shifts[1][...])
            back1 = jnp.concatenate([back1[:, :SIDE] + before[:, :SIDE], back1[:, SIDE:]], axis=1)
            back2 = jnp.concatenate([back2[:, :SIDE] + before[:, SIDE:], back2[:, SIDE:]], axis=1)
            tap = columns[:, 3 * e : 3 * e + 3]
            filtered.append(tap[:, 0:1] * x.astype(f32) + tap[:, 1:2] * back1 + tap[:, 2:3] * back2)
        product = (filtered[1] * filtered[2]).astype(bf16)
        owners = pl.ds(pl.multiple_of(blk * per_block, per_block), per_block)
        query[owners] = filtered[0].reshape(per_block, own, wide)
        direct[owners] = (columns[:, 9:10] * product.astype(f32)).reshape(per_block, own, wide)
        stacked = jnp.concatenate([product[:, s * SIDE : (s + 1) * SIDE] for s in range(s_lo)], axis=0)
        xsend[owners] = dot(order_x[...], stacked).astype(bf16).reshape(per_block, own * s_lo, SIDE)
        return carry

    lax.fori_loop(0, blocks, gate, 0)

    x_all = pltpu.make_async_remote_copy(
        src_ref=xsend.at[pl.ds(0, n - 1)], dst_ref=xbuf.at[pl.ds(0, n - 1)], send_sem=xsend_sem, recv_sem=xrecv_sem,
        device_id={"ctx": (me + 1) % n}, device_id_type=MESH,
    )

    def x_start(i, carry):
        d = at_peer(i)
        pltpu.make_async_remote_copy(
            src_ref=xsend.at[d], dst_ref=xbuf.at[me], send_sem=xsend_sem, recv_sem=xrecv_sem,
            device_id={"ctx": d}, device_id_type=MESH,
        ).start()
        return carry

    lax.fori_loop(1, n, x_start, 0)
    own_x = pltpu.make_async_copy(xsend.at[me], xbuf.at[me], own_sem.at[1])
    own_x.start()

    for chunk in range(1, len(chunks)):

        def f_start(i, carry, chunk=chunk):
            f_send(chunk, i)
            return carry

        lax.fori_loop(1, n, f_start, 0)

    for load in load_late:
        load.wait()
    own_x.wait()
    x_all.wait_recv()
    cos, sin = twiddle[0:SIDE, :], twiddle[SIDE : 2 * SIDE, :]

    for g in range(groups):
        taken = xbuf[:, g * xrows : (g + 1) * xrows, :].astype(f32)
        for k in range(2):
            block = taken[:, k * some * s_lo : (k + 1) * some * s_lo, :].reshape(n * some * s_lo, SIDE)
            turned[(2 * g + k) * SIDE : (2 * g + k + 1) * SIDE, :] = block.T.astype(bf16)

    def over_s(g, carry):
        rows = pl.ds(pl.multiple_of(g * 2 * SIDE, 2 * SIDE), 2 * SIDE)
        for c in range(some):
            part = dot(turned[rows, :], first[:, c * 2 * SIDE : (c + 1) * 2 * SIDE])
            lanes = slice(c % 2 * SIDE, (c % 2 + 1) * SIDE)
            for k in range(2):
                re, im = part[k * SIDE : (k + 1) * SIDE, :SIDE], part[k * SIDE : (k + 1) * SIDE, SIDE:]
                pair = g * some + k * 2 + c // 2
                spec[pair, 0:SIDE, lanes] = (re * cos + im * sin).astype(bf16)
                spec[pair, SIDE : 2 * SIDE, lanes] = (im * cos - re * sin).astype(bf16)
        return carry

    lax.fori_loop(0, groups, over_s, 0)

    def over_r(i, carry):
        for k in range(2):
            values[2 * i + k] = dot(forward[...], spec[2 * i + k])
        return carry

    lax.fori_loop(0, own // 4, over_r, 0, unroll=2)

    own_f.wait()

    def through(h, k):
        for j in range(2):
            pair = 2 * h + j
            taken = fbuf[:, pl.ds(pl.multiple_of(pair * 2 * cols, 2 * cols), 2 * cols), :].astype(f32)
            shaped = []
            for c in range(2):
                gains = taken[:, c * cols : (c + 1) * cols, :]
                lanes = slice(c * SIDE, (c + 1) * SIDE)
                straight = values[pair, 0:half, lanes].reshape(n, cols, SIDE) * gains
                crossed = values[pair, half : 2 * half, lanes].reshape(n, cols, SIDE) * gains
                shaped.append((straight + pltpu.roll(crossed, a_lo, 1)).reshape(half, SIDE).astype(bf16))
            part = dot(inverse[...], jnp.concatenate(shaped, axis=1))
            rows = pl.ds(pl.multiple_of(k * SIDE, SIDE), SIDE)
            for c in range(2):
                re, im = part[:SIDE, c * SIDE : (c + 1) * SIDE], part[SIDE:, c * SIDE : (c + 1) * SIDE]
                at = (2 * j + c) * 2 * SIDE
                back[rows, at : at + SIDE] = (re * cos - im * sin).astype(bf16)
                back[rows, at + SIDE : at + 2 * SIDE] = (re * sin + im * cos).astype(bf16)

    def y_copy(k, src, dst, d):
        rows = pl.ds(returns[k][0] * xrows, returns[k][1] * xrows)
        return pltpu.make_async_remote_copy(
            src_ref=ysend.at[src, rows], dst_ref=ybuf.at[dst, rows], send_sem=ysend_sem.at[k], recv_sem=yrecv_sem.at[k],
            device_id={"ctx": d}, device_id_type=MESH,
        )

    def y_all(k):
        return y_copy(k, pl.ds(0, n - 1), pl.ds(0, n - 1), (me + 1) % n)

    sends = {start + count - 1: k for k, (start, count) in enumerate(returns)}
    arrives = {start: chunk for chunk, (start, _) in enumerate(chunks)}
    own_y = []
    for g in range(groups):
        pairs = range(some * g, some * g + some)
        if pairs[0] in arrives:
            f_all(arrives[pairs[0]]).wait_recv()
        if pairs[2] in arrives:
            through(2 * g, 0)
            early = dot_nt(last[...], back[0:SIDE, :])
            f_all(arrives[pairs[2]]).wait_recv()
            through(2 * g + 1, 1)
            parts = [early, dot_nt(last[...], back[SIDE : 2 * SIDE, :])]
        else:

            def both(k, carry, g=g):
                through(2 * g + k, k)
                return carry

            lax.fori_loop(0, 2, both, 0, unroll=True)
            part = dot_nt(last[...], back[...])
            parts = [part[:, k * SIDE : (k + 1) * SIDE] for k in range(2)]
        part = jnp.concatenate([part.reshape(n, some * s_lo, SIDE) for part in parts], axis=1)
        ysend[:, g * xrows : (g + 1) * xrows, :] = part.astype(bf16)
        if g not in sends:
            continue

        def y_start(i, carry, k=sends[g]):
            d = at_peer(i)
            y_copy(k, d, me, d).start()
            return carry

        lax.fori_loop(1, n, y_start, 0)
        start, count = returns[sends[g]]
        mine = pl.ds(start * xrows, count * xrows)
        own_y.append(pltpu.make_async_copy(ysend.at[me, mine], ybuf.at[me, mine], own_sem.at[2 + sends[g]]))
        own_y[-1].start()

    owners = SIDE // GROUP
    for g in range(groups):
        for k, (start, _) in enumerate(returns):
            if g == start:
                own_y[k].wait()
                y_all(k).wait_recv()
        count = n // owners
        stacked = [
            ybuf[h * owners : (h + 1) * owners, g * xrows : (g + 1) * xrows, :].reshape(owners * xrows, SIDE) for h in range(count)
        ]
        arranged = dot(order_y[...], jnp.concatenate(stacked, axis=1))
        for h in range(count):
            for s in range(s_lo):
                conv[h * owners : (h + 1) * owners, g * GROUP : (g + 1) * GROUP, s * SIDE : (s + 1) * SIDE] = arranged[
                    s * SIDE : (s + 1) * SIDE, h * SIDE : (h + 1) * SIDE
                ].reshape(owners, GROUP, SIDE)
        if g % 2 == 1:
            rows = slice((g - 1) * GROUP, (g + 1) * GROUP)
            out[:, rows, :] = (query[:, rows, :] * (conv[:, rows, :] + direct[:, rows, :])).astype(bf16)

    halo.wait_send()
    x_all.wait_send()
    for chunk in range(len(chunks)):
        f_all(chunk).wait_send()
    for k in range(len(returns)):
        y_all(k).wait_send()


def shards(projections, short_filter, skip_gain, filter_spectra):
    n = lax.axis_size("ctx")
    channels, tokens = projections.shape[1:]
    freqs = filter_spectra.shape[2]
    own, s_lo, a_lo = channels // n, tokens // SIDE, freqs // SIDE
    groups = own // GROUP
    cols = 2 * a_lo
    pairs = own // 2
    chunks = [(0, pairs // 2), (pairs // 2, pairs // 4), (pairs * 3 // 4, pairs // 8), (pairs * 7 // 8, pairs // 8)]
    returns = [(0, groups * 3 // 4), (groups * 3 // 4, groups // 4)]
    hbm, vmem = pl.BlockSpec(memory_space=pltpu.HBM), pl.BlockSpec(memory_space=pltpu.VMEM)
    small, twiddle, first, last = tables(n, own, s_lo, a_lo)
    dma = pltpu.SemaphoreType.DMA
    operands = [
        filter_spectra, projections, jnp.swapaxes(short_filter, 1, 2), skip_gain.reshape(channels // SIDE, SIDE),
        *(jnp.asarray(table) for table in (small, twiddle, first, last)),
    ]
    return pl.pallas_call(
        functools.partial(kernel, n, own, s_lo, a_lo, chunks, returns),
        out_shape=jax.ShapeDtypeStruct((n, own, tokens), bf16),
        in_specs=[hbm] * 8,
        out_specs=vmem,
        scratch_shapes=[
            pltpu.VMEM(filter_spectra.shape, bf16),
            pltpu.VMEM(projections.shape, bf16),
            pltpu.VMEM((3, 3, channels), f32),
            pltpu.VMEM((channels // SIDE, SIDE), f32),
            pltpu.VMEM(small.shape, bf16),
            pltpu.VMEM(twiddle.shape, f32),
            pltpu.VMEM(first.shape, bf16),
            pltpu.VMEM(last.shape, bf16),
            pltpu.VMEM((n, own * cols, SIDE), bf16),
            pltpu.VMEM((n, own * cols, SIDE), bf16),
            pltpu.VMEM((n, own * s_lo, SIDE), bf16),
            pltpu.VMEM((n, own * s_lo, SIDE), bf16),
            pltpu.VMEM((n, own * s_lo, SIDE), bf16),
            pltpu.VMEM((n, own * s_lo, SIDE), bf16),
            pltpu.VMEM((2 * groups * SIDE, n * GROUP * s_lo // 2), bf16),
            pltpu.VMEM((own // 2, 2 * SIDE, 2 * SIDE), bf16),
            pltpu.VMEM((own // 2, 4 * SIDE, 2 * SIDE), f32),
            pltpu.VMEM((2 * SIDE, GROUP * SIDE), bf16),
            pltpu.VMEM((n, own, tokens), f32),
            pltpu.VMEM((n, own, tokens), f32),
            pltpu.VMEM((n, own, tokens), f32),
            pltpu.VMEM((16, channels), bf16),
            pltpu.VMEM((16, channels), bf16),
            dma((9,)),
            dma((2 + len(returns),)),
            dma((len(chunks),)),
            dma((len(chunks),)),
            dma,
            dma,
            dma((len(returns),)),
            dma((len(returns),)),
            dma,
            dma,
        ],
        compiler_params=pltpu.CompilerParams(collective_id=0, has_side_effects=True, vmem_limit_bytes=52 << 20),
        cost_estimate=pl.CostEstimate(flops=6_000_000_000, bytes_accessed=12_000_000, transcendentals=0),
    )(*(pltpu.with_memory_space_constraint(x, pltpu.HBM) for x in operands)).reshape(channels, tokens)


def solution(mesh):
    return jax.shard_map(
        shards,
        mesh=mesh,
        in_specs=(P(None, "ch", "ctx"), P(None, "ch", None), P("ch"), P(None, "ch", "ctx")),
        out_specs=P("ch", "ctx"),
        check_vma=False,
    )
```
